128 devices in a mesh: dp: 16 (over y, z_hi, core), tensor: 8 (over z_lo, x).
Axes of the slice: x: 4, y: 4, z: 4 (z_hi: 2, z_lo: 2; z = z_hi * 2 + z_lo), core: 2. Of those that a mesh axis runs over, the one named last changes fastest.
Arguments:
- tag_ids: int32 [128, 8], P(('dp', 'tensor')), may hold values from 0 to 127
- tag_amounts: float32 [128, 8], P(('dp', 'tensor')), may hold values from 0.05 to 1
- tag_table: bfloat16 [128, 256], replicated, may hold values from -6 to 6
- position_table: bfloat16 [32, 256], replicated, may hold values from -6 to 6
- prefix_weight: bfloat16 [256, 2048], replicated, may hold values from -0.75 to 0.75
- query_own: bfloat16 [128, 768, 4096], P('dp', None, 'tensor'), may hold values from -9 to 9
- key_own: bfloat16 [128, 768, 1024], P('dp', None, 'tensor'), may hold values from -6 to 6
- value_own: bfloat16 [128, 768, 1024], P('dp', None, 'tensor'), may hold values from -6 to 6
- out_grad: bfloat16 [128, 768, 4096], P('dp', None, 'tensor'), may hold values from -6 to 6
- seq_lengths: int32 [128], P('dp'), may hold values from 384 to 768, as said below
Outputs:
- attn_out: bfloat16 [128, 768, 4096], P('dp', None, 'tensor')
- prefix_grad: float32 [128, 32, 2048], P(('dp', 'tensor'))
- weight_grad: float32 [256, 2048], replicated
The draws below stay inside these ranges and needn't reach their ends.
Inputs may be any that keep to these rules, and one draw needn't show every extreme that they name: `seq_lengths`: some sequence is full in every draw.
All inputs are finite; a program needn't handle non-finite values.
Results may differ from the reference program's by a relative error of at most 0.0082.
Values may be sent and summed in bfloat16 or wider, within the bound.
A program may use at most 128 MiB of HBM per device.

```python
import math
import jax
import jax.numpy as jnp
from jax import lax

HD = 128
KVH = 8
HQ = 32
E = 256
NTAG = 128
P_SIZE = 32
L = 768
TAGS = 8
SEQS = 128


def draw_query_own(key, part):
    key = jax.random.fold_in(key, 5)
    normal_key = jax.random.fold_in(key, 0)
    values = jnp.clip(jax.random.normal(normal_key, (SEQS, L, HQ * HD), jnp.float32), -6.0, 6.0)
    return values.astype(jnp.bfloat16)


def draw_key_own(key, part):
    key = jax.random.fold_in(key, 9)
    values = jnp.clip(jax.random.normal(key, (SEQS, L, KVH * HD), jnp.float32), -6.0, 6.0)
    return values.astype(jnp.bfloat16)


def draw_seq_lengths(key, part):
    key = jax.random.fold_in(key, 7)
    lengths = jax.random.randint(key, (SEQS,), L // 2, L + 1, dtype=jnp.int32)
    return lengths.at[0].set(L)


def place_ends(result, own_key, low, high):
    spot = [jax.random.randint(jax.random.fold_in(own_key, axis), (), 0, length) for axis, length in enumerate(result.shape)]
    longest = result.shape.index(max(result.shape))
    beside = spot[:longest] + [(spot[longest] + 1) % result.shape[longest]] + spot[longest + 1:]
    return result.at[tuple(spot)].set(low).at[tuple(beside)].set(high)


def levels(key, shape, shards, smallest, largest):
    factor_of, own = 1.0, jax.random.fold_in(key, 6)
    for position, parts in shards:
        steps = jnp.exp(jax.random.uniform(jax.random.fold_in(own, position), (parts,), jnp.float32, smallest / len(shards), largest / len(shards)))
        factor_of = factor_of * jnp.repeat(steps, shape[position] // parts).reshape([-1 if axis == position else 1 for axis in range(len(shape))])
    return factor_of


def normal_values(stream_key, shape, scale, limit, shards=(), held_as=jnp.bfloat16):
    drawn = scale * jax.random.normal(stream_key, shape, jnp.float32)
    if shards:
        drawn = drawn * levels(stream_key, shape, shards, -0.22, 0.18)
    return jnp.clip(drawn, -limit, limit).astype(held_as)


def setup_inputs(seed: int = 0) -> dict:
    arg_keys = jax.random.split(jax.random.key(seed), 11)
    return {
        "tag_ids": place_ends(jax.random.randint(arg_keys[0], (SEQS, TAGS), 0, NTAG), jax.random.fold_in(arg_keys[0], 1), 0, NTAG - 1).astype(jnp.int32),
        "tag_amounts": jnp.clip(jnp.exp(math.log(1.0) - 2.9957323 * jax.random.uniform(arg_keys[1], (SEQS, TAGS), jnp.float32) ** levels(arg_keys[1], (SEQS, TAGS), ((0, 128),), -0.2, 0.2)), 0.05, 1.0),
        "tag_table": normal_values(arg_keys[2], (NTAG, E), 1.0, 6.0),
        "position_table": normal_values(arg_keys[3], (P_SIZE, E), 1.0, 6.0),
        "prefix_weight": normal_values(arg_keys[4], (E, KVH * 2 * HD), (E // 4) ** -0.5, 0.75),
        "query_own": draw_query_own(jax.random.fold_in(arg_keys[10], 71), 0),
        "key_own": draw_key_own(jax.random.fold_in(arg_keys[10], 71), 0),
        "value_own": normal_values(arg_keys[7], (SEQS, L, KVH * HD), 1.0, 6.0, ((0, 16), (2, 8))),
        "out_grad": normal_values(arg_keys[8], (SEQS, L, HQ * HD), 1.0, 6.0, ((0, 16), (2, 8))),
        "seq_lengths": draw_seq_lengths(jax.random.fold_in(arg_keys[10], 71), 0),
    }


def encode(tag_ids, tag_amounts, tag_table, position_table):
    onehot = (tag_ids[:, :, None] == jnp.arange(tag_table.shape[0], dtype=jnp.int32)[None, None, :]).astype(jnp.float32)
    mixture = jnp.sum(onehot * tag_amounts[:, :, None], axis=1) / jnp.sum(tag_amounts, axis=1)[:, None]
    pooled = jnp.dot(mixture, tag_table.astype(jnp.float32), precision=lax.Precision.HIGHEST)
    return jnp.tanh(position_table.astype(jnp.float32)[None, :, :] + pooled[:, None, :]).astype(jnp.bfloat16)


def attend(query, key_own, value_own, prefix, cotangent, length):
    row_count = query.shape[0]
    prefix_len = prefix.shape[0]
    shared_heads = key_own.shape[1] // HD
    group_size = query.shape[1] // (shared_heads * HD)
    score_scale = 1.0 / (HD ** 0.5)
    prefix_split = prefix.reshape(prefix_len, shared_heads, 2, HD).astype(jnp.float32)
    all_keys = jnp.concatenate([prefix_split[:, :, 0], key_own.reshape(row_count, shared_heads, HD).astype(jnp.float32)], 0)
    all_values = jnp.concatenate([prefix_split[:, :, 1], value_own.reshape(row_count, shared_heads, HD).astype(jnp.float32)], 0)
    query_heads = query.reshape(row_count, shared_heads, group_size, HD).astype(jnp.float32)
    scores = jnp.einsum('ikgd,jkd->kgij', query_heads, all_keys) * score_scale
    row_index = jnp.arange(row_count, dtype=jnp.int32)[:, None]
    col_index = jnp.arange(prefix_len + row_count, dtype=jnp.int32)[None, :] - prefix_len
    allowed = (col_index < 0) | ((col_index <= row_index) & (col_index < length))
    scores = jnp.where(allowed, scores, -1e30)
    row_max = jnp.max(scores, axis=-1, keepdims=True)
    exp_scores = jnp.exp(scores - row_max)
    probs = exp_scores / jnp.sum(exp_scores, axis=-1, keepdims=True)
    weights = probs.astype(jnp.bfloat16)
    output = jnp.einsum('kgij,jkd->ikgd', weights.astype(jnp.float32), all_values).astype(jnp.bfloat16)
    live_rows = (jnp.arange(row_count, dtype=jnp.int32) < length)[:, None, None, None]
    grad_live = jnp.where(live_rows, cotangent.reshape(row_count, shared_heads, group_size, HD), jnp.zeros((), jnp.bfloat16))
    row_delta = jnp.sum(grad_live.astype(jnp.float32) * output.astype(jnp.float32), axis=-1)
    row_delta = jnp.transpose(row_delta, (1, 2, 0))
    prob_grad = jnp.einsum('ikgd,jkd->kgij', grad_live.astype(jnp.float32), prefix_split[:, :, 1])
    score_grad = (probs[..., :prefix_len] * (prob_grad - row_delta[..., None])).astype(jnp.bfloat16)
    key_grad = jnp.einsum('kgij,ikgd->jkd', score_grad.astype(jnp.float32), query_heads) * score_scale
    value_grad = jnp.einsum('kgij,ikgd->jkd', weights[..., :prefix_len].astype(jnp.float32), grad_live.astype(jnp.float32))
    prefix_grads = jnp.stack([key_grad, value_grad], 2).reshape(prefix_len, shared_heads * 2 * HD)
    return output.reshape(row_count, -1), prefix_grads


def reference(tag_ids, tag_amounts, tag_table, position_table, prefix_weight, query_own, key_own, value_own, out_grad, seq_lengths):
    hidden = encode(tag_ids, tag_amounts, tag_table, position_table)
    example_count = hidden.shape[0]
    prefix = jnp.dot(hidden.reshape(-1, hidden.shape[2]), prefix_weight, preferred_element_type=jnp.float32)
    prefix = prefix.astype(jnp.bfloat16).reshape(example_count, hidden.shape[1], -1)

    def one_sequence(items):
        return attend(items[0], items[1], items[2], items[3], items[4], items[5])

    attn_out, prefix_grad = lax.map(one_sequence, (query_own, key_own, value_own, prefix, out_grad, seq_lengths))
    flat_hidden = hidden.reshape(-1, hidden.shape[2]).astype(jnp.float32)
    weight_grad = lax.dot_general(flat_hidden, prefix_grad.reshape(flat_hidden.shape[0], -1), (((0,), (0,)), ((), ())), precision=lax.Precision.HIGHEST)
    return attn_out, prefix_grad, weight_grad / example_count
```

```python
import functools
import jax
import jax.numpy as jnp
from jax import lax
from jax.experimental import pallas as pl
from jax.experimental.pallas import tpu as pltpu
from jax.sharding import PartitionSpec as P

HD = 128
F32 = jnp.float32
BF16 = jnp.bfloat16
LOG2E = 1.4426950408889634
NT = (((1,), (1,)), ((), ()))
TN = (((0,), (0,)), ((), ()))
MESH = pl.DeviceIdType.MESH


def dot(a, b, dims=(((1,), (0,)), ((), ()))):
    return lax.dot_general(a, b, dims, preferred_element_type=F32)


def encode_kernel(n, ids_hbm, amt_hbm, table_hbm, pos_hbm, weight_hbm, prefix_ref, hidden_ref,
                  ids_ref, amt_ref, table_ref, pos_ref, wbuf, mine, got, send_sem, recv_sem, load_sem):
    d, t = lax.axis_index("dp"), lax.axis_index("tensor")
    barrier = pltpu.get_barrier_semaphore()
    for i in range(1, n):
        pl.semaphore_signal(barrier, inc=1, device_id=(d, lax.rem(t + i, n)), device_id_type=MESH)
    cols = wbuf.shape[1]
    loads = [pltpu.make_async_copy(src, dst, load_sem.at[i]) for i, (src, dst) in enumerate((
        (ids_hbm, ids_ref), (amt_hbm, amt_ref), (table_hbm, table_ref), (pos_hbm, pos_ref),
        (weight_hbm.at[:, pl.ds(pl.multiple_of(t * cols, cols), cols)], wbuf)))]
    for load in loads:
        load.start()
    loads[0].wait()
    loads[1].wait()
    tags = table_ref.shape[0]
    lane = lax.broadcasted_iota(jnp.int32, (1, tags), 1)
    ids, amounts = ids_ref[...], amt_ref[...]
    mix = jnp.zeros((1, tags), F32)
    for k in range(ids.shape[1]):
        mix += jnp.where(ids[:, k:k + 1] == lane, amounts[:, k:k + 1], 0.0)
    mix = mix / jnp.sum(amounts, axis=1, keepdims=True)
    mine[...] = jnp.broadcast_to(mix, mine.shape)
    got[t] = jnp.broadcast_to(mix, mine.shape)
    pl.semaphore_wait(barrier, n - 1)
    copies = []
    for i in range(1, n):
        copy = pltpu.make_async_remote_copy(
            src_ref=mine, dst_ref=got.at[t], send_sem=send_sem.at[i], recv_sem=recv_sem.at[i],
            device_id=(d, lax.rem(t + i, n)), device_id_type=MESH)
        copy.start()
        copies.append(copy)
    for load in loads[2:]:
        load.wait()
    for copy in copies:
        copy.wait()
    mixture = jnp.concatenate([got[j, 0:1] for j in range(n)], 0)
    pooled = jnp.dot(mixture, table_ref[...].astype(F32), precision=lax.Precision.HIGHEST,
                     preferred_element_type=F32)
    pos = pos_ref[...].astype(F32)
    hidden = jnp.concatenate([jnp.tanh(pos + pooled[j:j + 1]) for j in range(n)], 0).astype(BF16)
    hidden_ref[...] = hidden
    prefix_ref[...] = dot(hidden, wbuf[...]).astype(BF16).reshape(prefix_ref.shape)


def encode(tag_ids, tag_amounts, tag_table, position_table, prefix_weight):
    n = lax.axis_size("tensor")
    width, total = prefix_weight.shape
    plen = position_table.shape[0]
    vmem = pl.BlockSpec(memory_space=pltpu.VMEM)
    return pl.pallas_call(
        functools.partial(encode_kernel, n),
        out_shape=(jax.ShapeDtypeStruct((n, plen, total // n), BF16),
                   jax.ShapeDtypeStruct((n * plen, width), BF16)),
        in_specs=[pl.BlockSpec(memory_space=pltpu.HBM)] * 5,
        out_specs=(vmem, vmem),
        scratch_shapes=[
            pltpu.VMEM(tag_ids.shape, jnp.int32),
            pltpu.VMEM(tag_amounts.shape, F32),
            pltpu.VMEM(tag_table.shape, BF16),
            pltpu.VMEM(position_table.shape, BF16),
            pltpu.VMEM((width, total // n), BF16),
            pltpu.VMEM((8, tag_table.shape[0]), F32),
            pltpu.VMEM((n, 8, tag_table.shape[0]), F32),
            pltpu.SemaphoreType.DMA((n,)),
            pltpu.SemaphoreType.DMA((n,)),
            pltpu.SemaphoreType.DMA((5,)),
        ],
        compiler_params=pltpu.CompilerParams(collective_id=0, has_side_effects=True, vmem_limit_bytes=56 * 1024 * 1024),
    )(tag_ids, tag_amounts, tag_table, position_table, prefix_weight)


def attend_kernel(NR, len_ref, q_ref, k_ref, v_ref, g_ref, pre_ref, out_ref, pg_ref,
                  vx, pkbd, pvbd, ds_scr, w_scr, pp_scr, bad_scr):
    step = pl.program_id(0)
    length = len_ref[step]
    rows = q_ref.shape[1]
    heads = q_ref.shape[2] // HD
    plen = pre_ref.shape[1]
    seg_w = heads * plen
    scale = 1.0 / HD**0.5

    @pl.when(step == 0)
    def _():
        pkbd[...] = jnp.zeros_like(pkbd)
        pvbd[...] = jnp.zeros_like(pvbd)
        for h in range(heads):
            pvbd[h * plen:(h + 1) * plen, (heads + h) * HD:(heads + h + 1) * HD] = jnp.full((plen, HD), -1.0, BF16)
        vx[0:seg_w, HD:] = jnp.ones((seg_w, HD), BF16)

    pk = pre_ref[0, :, :HD]
    pv = pre_ref[0, :, HD:]
    for h in range(heads):
        pkbd[h * plen:(h + 1) * plen, h * HD:(h + 1) * HD] = pk
        pvbd[h * plen:(h + 1) * plen, h * HD:(h + 1) * HD] = pv
        vx[h * plen:(h + 1) * plen, :HD] = pv
    live = lax.broadcasted_iota(jnp.int32, (rows, HD), 0) < length
    vx[seg_w:, :HD] = jnp.where(live, v_ref[0].astype(F32), 0.0).astype(BF16)
    vx[seg_w:, HD:] = jnp.where(live, 1.0, 0.0).astype(BF16)

    seg = lax.broadcasted_iota(jnp.int32, (NR, seg_w), 1) // plen
    causal = (lax.broadcasted_iota(jnp.int32, (heads * NR, NR), 1)
              <= lax.broadcasted_iota(jnp.int32, (heads * NR, NR), 0) % NR)
    c = scale * LOG2E

    def grads(r0, nr, probs, g, out):
        go = (g.astype(F32) * out.astype(F32)).astype(BF16)
        diff = dot(g, pvbd[:, :heads * HD], NT) + dot(go, pvbd[:, heads * HD:], NT)
        alive = lax.broadcasted_iota(jnp.int32, (nr, seg_w), 0) + r0 < length
        ds_scr[pl.ds(r0, nr)] = jnp.where(alive, probs * diff, 0.0).astype(BF16)
        w_scr[pl.ds(r0, nr)] = jnp.where(alive, probs, 0.0).astype(BF16)

    def finish():
        dk = dot(ds_scr[...], q_ref[0], TN)
        dv = dot(w_scr[...], g_ref[0], TN)
        pg_ref[0, :, :HD] = sum(dk[h * plen:(h + 1) * plen, h * HD:(h + 1) * HD] for h in range(heads)) * scale
        pg_ref[0, :, HD:] = sum(dv[h * plen:(h + 1) * plen, h * HD:(h + 1) * HD] for h in range(heads))

    bad = jnp.zeros((8, HD), F32)
    for r0 in range(0, rows, NR):
        qr = q_ref[0, r0:r0 + NR]
        q4 = jnp.concatenate([qr[:, h * HD:(h + 1) * HD] for h in range(heads)], 0)
        pp = jnp.exp2(dot(qr, pkbd[...], NT) * c)
        ppb = pp.astype(BF16)
        zero = jnp.zeros_like(ppb)
        parts = [jnp.concatenate([jnp.where(seg == h, ppb, zero) for h in range(heads)], 0)]
        if r0:
            parts.append(jnp.exp2(dot(q4, k_ref[0, :r0], NT) * c).astype(BF16))
        diag = jnp.exp2(dot(q4, k_ref[0, r0:r0 + NR], NT) * c)
        parts.append(jnp.where(causal, diag, 0.0).astype(BF16))
        p = jnp.concatenate(parts, 1)
        o = dot(p, vx[:seg_w + r0 + NR])
        sums = o[:, HD:]
        ok = (sums > 1e-25) & (sums < 1e25)
        bad = jnp.maximum(bad, jnp.max(jnp.where(ok, 0.0, 1.0).reshape(-1, 8, HD), axis=0))
        inv = 1.0 / sums
        o = (o[:, :HD] * inv).astype(BF16)
        inv_seg = inv[:NR]
        for h in range(1, heads):
            inv_seg = jnp.where(seg == h, inv[h * NR:(h + 1) * NR], inv_seg)
        out = jnp.concatenate([o[h * NR:(h + 1) * NR] for h in range(heads)], 1)
        out_ref[0, r0:r0 + NR] = out
        grads(r0, NR, pp * inv_seg, g_ref[0, r0:r0 + NR], out)
    finish()

    @pl.when(jnp.max(bad) > 0.0)
    def _():
        nr = HD
        seg1 = lax.broadcasted_iota(jnp.int32, (nr, seg_w), 1) // plen

        def block(r, carry):
            r0 = pl.multiple_of(r * nr, nr)
            sp_all = dot(q_ref[0, pl.ds(r0, nr)], pkbd[...], NT) * scale
            row = lax.broadcasted_iota(jnp.int32, (nr, rows), 0) + r0
            col = lax.broadcasted_iota(jnp.int32, (nr, rows), 1)
            seen = (col <= row) & (col < length)
            pp_scr[...] = jnp.zeros_like(pp_scr)

            def head(h, carry):
                lanes = pl.ds(pl.multiple_of(h * HD, HD), HD)
                s = dot(q_ref[0, pl.ds(r0, nr), lanes], k_ref[0], NT) * scale
                s = jnp.where(seen, s, -1e30)
                sp = jnp.where(seg1 == h, sp_all, -1e30)
                m = jnp.maximum(jnp.max(s, axis=1, keepdims=True), jnp.max(sp, axis=1, keepdims=True))
                p = jnp.exp(s - m)
                p_pre = jnp.exp(sp - m)
                inv = 1.0 / (jnp.sum(p, axis=1, keepdims=True) + jnp.sum(p_pre, axis=1, keepdims=True))
                p_pre = p_pre * inv
                o = (dot((p * inv).astype(BF16), vx[seg_w:, :HD])
                     + dot(p_pre.astype(BF16), vx[:seg_w, :HD]))
                out_ref[0, pl.ds(r0, nr), lanes] = o.astype(BF16)
                pp_scr[...] += p_pre
                return carry

            lax.fori_loop(0, heads, head, 0)
            grads(r0, nr, pp_scr[...], g_ref[0, pl.ds(r0, nr)], out_ref[0, pl.ds(r0, nr)])
            return carry

        lax.fori_loop(0, rows // nr, block, 0)
        finish()


def attention(lengths, q, k, v, g, prefix, NR=256):
    n, rows, width = q.shape
    heads = width // HD
    plen = prefix.shape[1]
    seg_w = heads * plen
    spec = lambda shape: pl.BlockSpec((1,) + shape, lambda e: (e, 0, 0))
    return pl.pallas_call(
        functools.partial(attend_kernel, NR),
        grid=(n,),
        out_shape=(jax.ShapeDtypeStruct(q.shape, BF16), jax.ShapeDtypeStruct((n, plen, 2 * HD), F32)),
        in_specs=[pl.BlockSpec(memory_space=pltpu.SMEM), spec((rows, width)), spec((rows, HD)), spec((rows, HD)),
                  spec((rows, width)), spec((plen, 2 * HD))],
        out_specs=(spec((rows, width)), spec((plen, 2 * HD))),
        scratch_shapes=[
            pltpu.VMEM((seg_w + rows, 2 * HD), BF16),
            pltpu.VMEM((seg_w, width), BF16),
            pltpu.VMEM((seg_w, 2 * width), BF16),
            pltpu.VMEM((rows, seg_w), BF16),
            pltpu.VMEM((rows, seg_w), BF16),
            pltpu.VMEM((HD, seg_w), F32),
            pltpu.VMEM((8, HD), F32),
        ],
        compiler_params=pltpu.CompilerParams(vmem_limit_bytes=56 * 1024 * 1024),
    )(lengths, q, k, v, g, prefix)


def exchange_kernel(hidden_ref, pg_ref, own_ref, all_ref,
                    out_buf, part, landed, sems_pg, sems_rs, sems_ag):
    d, t = lax.axis_index("dp"), lax.axis_index("tensor")
    y, zh, core = d // 4, lax.rem(d // 2, 2), lax.rem(d, 2)
    zl, x = t // 4, lax.rem(t, 4)
    z = zh * 2 + zl

    def device(x, y, z, core):
        return ((y * 2 + z // 2) * 2 + core, lax.rem(z, 2) * 4 + x)

    barrier = pltpu.get_barrier_semaphore()
    nt, nd = 8, 16
    peers = [(d, lax.rem(t + i, nt)) for i in range(1, nt)]
    peers += [(lax.rem(d + i, nd), t) for i in range(1, nd)]
    peers += [device(x, y, lax.rem(z + i, 4), core) for i in range(1, 4)]
    for peer in peers:
        pl.semaphore_signal(barrier, inc=1, device_id=peer, device_id_type=MESH)

    pg = pg_ref[...]
    high = pg.astype(BF16)
    out_buf[...] = high
    flat = pg.reshape(-1, pg.shape[2])
    flat_high = high.reshape(flat.shape)
    low = (flat - flat_high.astype(F32)).astype(BF16)
    hidden = hidden_ref[...]
    total = dot(hidden, flat_high, TN) + dot(hidden, low, TN)
    part[...] = total.astype(BF16).reshape(part.shape)
    own_ref[t] = out_buf[t]
    pl.semaphore_wait(barrier, len(peers))

    def send(src, dst, sems, i, peer):
        copy = pltpu.make_async_remote_copy(
            src_ref=src, dst_ref=dst, send_sem=sems.at[0, i], recv_sem=sems.at[1, i],
            device_id=peer, device_id_type=MESH)
        copy.start()
        return copy

    rs = []
    for i in range(1, nd):
        to = lax.rem(d + i, nd)
        rs.append(send(part.at[to], landed.at[i], sems_rs, i, (to, t)))
    a2a = []
    for i in range(1, nt):
        to = lax.rem(t + i, nt)
        a2a.append(send(out_buf.at[to], own_ref.at[t], sems_pg, i, (d, to)))
    chunk = part[d].astype(F32)
    for i, copy in enumerate(rs):
        copy.wait()
        chunk += landed[i + 1].astype(F32)
    all_ref[core, z, y, x] = (chunk * (1.0 / 128)).astype(BF16)
    pending = []
    for phase, (block, peer) in enumerate((
            (all_ref.at[core, z, y, x], lambda i: device(lax.rem(x + i, 4), y, z, core)),
            (all_ref.at[core, z, y], lambda i: device(x, lax.rem(y + i, 4), z, core)),
            (all_ref.at[core, z], lambda i: device(x, y, lax.rem(z + i, 4), core)))):
        copies = [send(block, block, sems_ag, phase * 4 + i, peer(i)) for i in range(1, 4)]
        for copy in copies:
            copy.wait()
    last = send(all_ref.at[core], all_ref.at[core], sems_ag, 0, device(x, y, z, 1 - core))
    last.wait()
    for copy in a2a:
        copy.wait()


def exchange(hidden, pgrads):
    n, plen, cols = pgrads.shape
    width = hidden.shape[1]
    nd = 16
    vmem = pl.BlockSpec(memory_space=pltpu.VMEM)
    return pl.pallas_call(
        exchange_kernel,
        out_shape=(jax.ShapeDtypeStruct((n, plen, cols), BF16),
                   jax.ShapeDtypeStruct((2, 4, 4, 4, width // nd, cols), BF16)),
        in_specs=[vmem, vmem],
        out_specs=(vmem, vmem),
        scratch_shapes=[
            pltpu.VMEM((n, plen, cols), BF16),
            pltpu.VMEM((nd, width // nd, cols), BF16),
            pltpu.VMEM((nd, width // nd, cols), BF16),
            pltpu.SemaphoreType.DMA((2, n)),
            pltpu.SemaphoreType.DMA((2, nd)),
            pltpu.SemaphoreType.DMA((2, 12)),
        ],
        compiler_params=pltpu.CompilerParams(collective_id=1, has_side_effects=True, vmem_limit_bytes=56 * 1024 * 1024),
    )(hidden, pgrads)


def finish_kernel(own_ref, all_ref, prefix_grad_ref, weight_grad_ref):
    cols = own_ref.shape[2]
    for j in range(own_ref.shape[0]):
        prefix_grad_ref[0, :, j * cols:(j + 1) * cols] = own_ref[j].astype(F32)
    rows = all_ref.shape[4]
    for core in range(2):
        for z in range(4):
            r0 = ((z // 2) * 2 + core) * rows
            for x in range(4):
                c0 = ((z % 2) * 4 + x) * cols
                weight_grad_ref[r0:r0 + rows, c0:c0 + cols] = all_ref[core, z, 0, x].astype(F32)


def finish(own, gathered):
    n, plen, cols = own.shape
    rows = gathered.shape[4]
    return pl.pallas_call(
        finish_kernel,
        grid=(4,),
        out_shape=(jax.ShapeDtypeStruct((1, plen, n * cols), F32),
                   jax.ShapeDtypeStruct((16 * rows, n * cols), F32)),
        in_specs=[pl.BlockSpec((n // 4, plen, cols), lambda y: (y, 0, 0)),
                  pl.BlockSpec((2, 4, 1, 4, rows, cols), lambda y: (0, 0, y, 0, 0, 0))],
        out_specs=(pl.BlockSpec((1, plen, n // 4 * cols), lambda y: (0, 0, y)),
                   pl.BlockSpec((4 * rows, n * cols), lambda y: (y, 0))),
        compiler_params=pltpu.CompilerParams(vmem_limit_bytes=56 * 1024 * 1024),
    )(own, gathered)


def shards(tag_ids, tag_amounts, tag_table, position_table, prefix_weight,
           query_own, key_own, value_own, out_grad, seq_lengths):
    prefix, hidden = encode(tag_ids, tag_amounts, tag_table, position_table, prefix_weight)
    attn_out, pgrads = attention(seq_lengths, query_own, key_own, value_own, out_grad, prefix)
    prefix_grad, weight_grad = finish(*exchange(hidden, pgrads))
    return attn_out, prefix_grad, weight_grad


def solution(mesh):
    return jax.shard_map(
        shards,
        mesh=mesh,
        in_specs=(
            P(("dp", "tensor"), None),
            P(("dp", "tensor"), None),
            P(),
            P(),
            P(),
            P("dp", None, "tensor"),
            P("dp", None, "tensor"),
            P("dp", None, "tensor"),
            P("dp", None, "tensor"),
            P("dp"),
        ),
        out_specs=(P("dp", None, "tensor"), P(("dp", "tensor"), None, None), P()),
        check_vma=False,
    )
```

```python
import functools
import jax
import jax.numpy as jnp
from jax import lax
from jax.experimental import pallas as pl
from jax.experimental.pallas import tpu as pltpu
from jax.sharding import PartitionSpec as P

HD = 128
SEQS = 128
F32 = jnp.float32
BF16 = jnp.bfloat16
LOG2E = 1.4426950408889634
NT = (((1,), (1,)), ((), ()))
TN = (((0,), (0,)), ((), ()))
MESH = pl.DeviceIdType.MESH


def dot(a, b, dims=(((1,), (0,)), ((), ()))):
    return lax.dot_general(a, b, dims, preferred_element_type=F32)


def encode_kernel(n, ids_hbm, amt_hbm, table_hbm, pos_hbm, weight_hbm, prefix_ref, hidden_ref,
                  ids_ref, amt_ref, table_ref, pos_ref, wbuf, mine, got, send_sem, recv_sem, load_sem):
    d, t = lax.axis_index("dp"), lax.axis_index("tensor")
    barrier = pltpu.get_barrier_semaphore()
    for i in range(1, n):
        pl.semaphore_signal(barrier, inc=1, device_id=(d, lax.rem(t + i, n)), device_id_type=MESH)
    cols = wbuf.shape[1]
    loads = [pltpu.make_async_copy(src, dst, load_sem.at[i]) for i, (src, dst) in enumerate((
        (ids_hbm, ids_ref), (amt_hbm, amt_ref), (table_hbm, table_ref), (pos_hbm, pos_ref),
        (weight_hbm.at[:, pl.ds(pl.multiple_of(t * cols, cols), cols)], wbuf)))]
    for load in loads:
        load.start()
    loads[0].wait()
    loads[1].wait()
    tags = table_ref.shape[0]
    lane = lax.broadcasted_iota(jnp.int32, (1, tags), 1)
    ids, amounts = ids_ref[...], amt_ref[...]
    mix = jnp.zeros((1, tags), F32)
    for k in range(ids.shape[1]):
        mix += jnp.where(ids[:, k:k + 1] == lane, amounts[:, k:k + 1], 0.0)
    mix = mix / jnp.sum(amounts, axis=1, keepdims=True)
    mine[...] = jnp.broadcast_to(mix, mine.shape)
    got[t] = jnp.broadcast_to(mix, mine.shape)
    pl.semaphore_wait(barrier, n - 1)
    copies = []
    for i in range(1, n):
        copy = pltpu.make_async_remote_copy(
            src_ref=mine, dst_ref=got.at[t], send_sem=send_sem.at[i], recv_sem=recv_sem.at[i],
            device_id=(d, lax.rem(t + i, n)), device_id_type=MESH)
        copy.start()
        copies.append(copy)
    for load in loads[2:]:
        load.wait()
    for copy in copies:
        copy.wait()
    mixture = jnp.concatenate([got[j, 0:1] for j in range(n)], 0)
    pooled = jnp.dot(mixture, table_ref[...].astype(F32), precision=lax.Precision.HIGHEST,
                     preferred_element_type=F32)
    pos = pos_ref[...].astype(F32)
    hidden = jnp.concatenate([jnp.tanh(pos + pooled[j:j + 1]) for j in range(n)], 0).astype(BF16)
    hidden_ref[...] = hidden
    prefix_ref[...] = dot(hidden, wbuf[...]).astype(BF16).reshape(prefix_ref.shape)


def encode(tag_ids, tag_amounts, tag_table, position_table, prefix_weight):
    n = lax.axis_size("tensor")
    width, total = prefix_weight.shape
    plen = position_table.shape[0]
    vmem = pl.BlockSpec(memory_space=pltpu.VMEM)
    return pl.pallas_call(
        functools.partial(encode_kernel, n),
        out_shape=(jax.ShapeDtypeStruct((n, plen, total // n), BF16),
                   jax.ShapeDtypeStruct((n * plen, width), BF16)),
        in_specs=[pl.BlockSpec(memory_space=pltpu.HBM)] * 5,
        out_specs=(vmem, vmem),
        scratch_shapes=[
            pltpu.VMEM(tag_ids.shape, jnp.int32),
            pltpu.VMEM(tag_amounts.shape, F32),
            pltpu.VMEM(tag_table.shape, BF16),
            pltpu.VMEM(position_table.shape, BF16),
            pltpu.VMEM((width, total // n), BF16),
            pltpu.VMEM((8, tag_table.shape[0]), F32),
            pltpu.VMEM((n, 8, tag_table.shape[0]), F32),
            pltpu.SemaphoreType.DMA((n,)),
            pltpu.SemaphoreType.DMA((n,)),
            pltpu.SemaphoreType.DMA((5,)),
        ],
        compiler_params=pltpu.CompilerParams(collective_id=0, has_side_effects=True, vmem_limit_bytes=56 * 1024 * 1024),
        name="encode",
    )(tag_ids, tag_amounts, tag_table, position_table, prefix_weight)


def attend_kernel(NR, GROUPS, LATE, len_ref, q_ref, k_ref, v_ref, g_ref, pre_ref, out_ref, pg_ref,
                  vx, pkbd, pvbd, ds_scr, w_scr, pp_scr):
    step = pl.program_id(0)
    length = len_ref[step]
    rows = q_ref.shape[1]
    heads = q_ref.shape[2] // HD
    plen = pre_ref.shape[1]
    seg_w = heads * plen
    scale = 1.0 / HD**0.5

    @pl.when(step == 0)
    def _():
        pkbd[...] = jnp.zeros_like(pkbd)
        pvbd[...] = jnp.zeros_like(pvbd)
        vx[0:seg_w, HD:] = jnp.ones((seg_w, HD), BF16)

    pk = pre_ref[0, :, :HD]
    pv = pre_ref[0, :, HD:]
    for h in range(heads):
        pkbd[h * plen:(h + 1) * plen, h * HD:(h + 1) * HD] = pk
        pvbd[h * plen:(h + 1) * plen, h * HD:(h + 1) * HD] = pv
        vx[h * plen:(h + 1) * plen, :HD] = pv
    live = lax.broadcasted_iota(jnp.int32, (rows, HD), 0) < length
    vx[seg_w:, :HD] = jnp.where(live, v_ref[0].astype(F32), 0.0).astype(BF16)
    vx[seg_w:, HD:] = jnp.where(live, 1.0, 0.0).astype(BF16)

    seg = lax.broadcasted_iota(jnp.int32, (NR, seg_w), 1) // plen
    c = scale * LOG2E

    per = heads // GROUPS
    causal = (lax.broadcasted_iota(jnp.int32, (per * NR, NR), 1)
              <= lax.broadcasted_iota(jnp.int32, (per * NR, NR), 0) % NR)

    def score_phase(r0):
        qr = q_ref[0, r0:r0 + NR]
        pp = jnp.exp2(dot(qr, pkbd[...], NT) * c)
        ppb = pp.astype(BF16)
        zero = jnp.zeros_like(ppb)
        ps = []
        for j in range(GROUPS):
            hs = range(j * per, (j + 1) * per)
            q4 = jnp.concatenate([qr[:, h * HD:(h + 1) * HD] for h in hs], 0)
            parts = [jnp.concatenate([jnp.where(seg == h, ppb, zero) for h in hs], 0)]
            if r0:
                parts.append(jnp.exp2(dot(q4, k_ref[0, :r0], NT) * c).astype(BF16))
            diag = jnp.exp2(dot(q4, k_ref[0, r0:r0 + NR], NT) * c)
            parts.append(jnp.where(causal, diag, 0.0).astype(BF16))
            ps.append(jnp.concatenate(parts, 1))
        return pp, ps

    def value_phase(r0, pp, ps, bad):
        invs = []
        os = [dot(p, vx[:seg_w + r0 + NR]) for p in ps]
        for j, o in enumerate(os):
            sums = o[:, HD:]
            ok = (sums > 1e-25) & (sums < 1e25)
            bad = jnp.maximum(bad, jnp.max(jnp.where(ok, 0.0, 1.0).reshape(-1, 8, HD), axis=0))
            inv = 1.0 / sums
            o = (o[:, :HD] * inv).astype(BF16)
            for i in range(per):
                h = j * per + i
                invs.append(inv[i * NR:(i + 1) * NR])
                out_ref[0, r0:r0 + NR, h * HD:(h + 1) * HD] = o[i * NR:(i + 1) * NR]
        inv_seg = invs[0]
        for h in range(1, heads):
            inv_seg = jnp.where(seg == h, invs[h], inv_seg)
        probs = pp * inv_seg
        alive = lax.broadcasted_iota(jnp.int32, (NR, seg_w), 0) + r0 < length
        probs = jnp.where(alive, probs, 0.0)
        w_scr[r0:r0 + NR] = probs.astype(BF16)
        pp_scr[r0:r0 + NR] = probs
        return bad

    def row_delta(g, out, seg_r):
        delta = None
        for h in range(heads):
            lanes = slice(h * HD, (h + 1) * HD)
            total = jnp.sum(g[:, lanes].astype(F32) * out[:, lanes].astype(F32), axis=1, keepdims=True)
            delta = jnp.broadcast_to(total, seg_r.shape) if h == 0 else jnp.where(seg_r == h, total, delta)
        return delta

    def grad_phase(r0, nr, probs):
        g = g_ref[0, r0:r0 + nr]
        seg_r = lax.broadcasted_iota(jnp.int32, (nr, seg_w), 1) // plen
        delta = row_delta(g, out_ref[0, r0:r0 + nr], seg_r)
        ds_scr[r0:r0 + nr] = (probs * (dot(g, pvbd[...], NT) - delta)).astype(BF16)

    def finish():
        w = 2 * HD
        for half in range(heads // 2):
            lanes = slice(half * w, (half + 1) * w)
            dk = dot(ds_scr[...], q_ref[0, :, lanes], TN)
            dv = dot(w_scr[...], g_ref[0, :, lanes], TN)
            for i in range(2):
                h = half * 2 + i
                a = dk[h * plen:(h + 1) * plen, i * HD:(i + 1) * HD] * scale
                b = dv[h * plen:(h + 1) * plen, i * HD:(i + 1) * HD]
                if h:
                    a, b = a + pa, b + pb
                pa, pb = a, b
        pg_ref[0, :, :HD] = pa
        pg_ref[0, :, HD:] = pb

    bad = jnp.zeros((8, HD), F32)
    starts = list(range(0, rows, NR))
    state = score_phase(starts[0])
    for i, r0 in enumerate(starts):
        now = state
        if i + 1 < len(starts):
            state = score_phase(starts[i + 1])
        bad = value_phase(r0, *now, bad)
    step_rows = rows // LATE
    for r0 in range(0, rows, step_rows):
        grad_phase(r0, step_rows, pp_scr[r0:r0 + step_rows])
    finish()

    @pl.when(jnp.max(bad) > 0.0)
    def _():
        nr = HD
        seg1 = lax.broadcasted_iota(jnp.int32, (nr, seg_w), 1) // plen

        def block(r, carry):
            r0 = pl.multiple_of(r * nr, nr)
            sp_all = dot(q_ref[0, pl.ds(r0, nr)], pkbd[...], NT) * scale
            row = lax.broadcasted_iota(jnp.int32, (nr, rows), 0) + r0
            col = lax.broadcasted_iota(jnp.int32, (nr, rows), 1)
            seen = (col <= row) & (col < length)
            pp_scr[pl.ds(r0, nr)] = jnp.zeros((nr, seg_w), F32)

            def head(h, carry):
                lanes = pl.ds(pl.multiple_of(h * HD, HD), HD)
                s = dot(q_ref[0, pl.ds(r0, nr), lanes], k_ref[0], NT) * scale
                s = jnp.where(seen, s, -1e30)
                sp = jnp.where(seg1 == h, sp_all, -1e30)
                m = jnp.maximum(jnp.max(s, axis=1, keepdims=True), jnp.max(sp, axis=1, keepdims=True))
                p = jnp.exp(s - m)
                p_pre = jnp.exp(sp - m)
                inv = 1.0 / (jnp.sum(p, axis=1, keepdims=True) + jnp.sum(p_pre, axis=1, keepdims=True))
                p_pre = p_pre * inv
                o = (dot((p * inv).astype(BF16), vx[seg_w:, :HD])
                     + dot(p_pre.astype(BF16), vx[:seg_w, :HD]))
                out_ref[0, pl.ds(r0, nr), lanes] = o.astype(BF16)
                pp_scr[pl.ds(r0, nr)] += p_pre
                return carry

            lax.fori_loop(0, heads, head, 0)
            alive = lax.broadcasted_iota(jnp.int32, (nr, seg_w), 0) + r0 < length
            probs = jnp.where(alive, pp_scr[pl.ds(r0, nr)], 0.0)
            w_scr[pl.ds(r0, nr)] = probs.astype(BF16)
            g = g_ref[0, pl.ds(r0, nr)]
            delta = row_delta(g, out_ref[0, pl.ds(r0, nr)], seg1)
            ds_scr[pl.ds(r0, nr)] = (probs * (dot(g, pvbd[...], NT) - delta)).astype(BF16)
            return carry

        lax.fori_loop(0, rows // nr, block, 0)
        finish()


def attention(lengths, q, k, v, g, prefix, NR=128, GROUPS=2, LATE=2):
    n, rows, width = q.shape
    heads = width // HD
    plen = prefix.shape[1]
    seg_w = heads * plen
    spec = lambda shape: pl.BlockSpec((1,) + shape, lambda e: (e, 0, 0))
    return pl.pallas_call(
        functools.partial(attend_kernel, NR, GROUPS, LATE),
        grid=(n,),
        out_shape=(jax.ShapeDtypeStruct(q.shape, BF16), jax.ShapeDtypeStruct((n, plen, 2 * HD), F32)),
        in_specs=[pl.BlockSpec(memory_space=pltpu.SMEM), spec((rows, width)), spec((rows, HD)), spec((rows, HD)),
                  spec((rows, width)), spec((plen, 2 * HD))],
        out_specs=(spec((rows, width)), spec((plen, 2 * HD))),
        scratch_shapes=[
            pltpu.VMEM((seg_w + rows, 2 * HD), BF16),
            pltpu.VMEM((seg_w, width), BF16),
            pltpu.VMEM((seg_w, width), BF16),
            pltpu.VMEM((rows, seg_w), BF16),
            pltpu.VMEM((rows, seg_w), BF16),
            pltpu.VMEM((rows, seg_w), F32),
        ],
        compiler_params=pltpu.CompilerParams(vmem_limit_bytes=56 * 1024 * 1024),
        name="attend",
    )(lengths, q, k, v, g, prefix)


def exchange_kernel(hid_hbm, pg_hbm, own_ref, all_ref, hid, pg, out_buf, part, landed,
                    load_sem, sems_pg, sems_rs, sems_ag, sems_core):
    d, t = lax.axis_index("dp"), lax.axis_index("tensor")
    y, zh, core = d // 4, lax.rem(d // 2, 2), lax.rem(d, 2)
    zl, x = t // 4, lax.rem(t, 4)
    z = zh * 2 + zl
    me = dict(x=x, y=y, z=z)

    def device(x, y, z, core):
        return ((y * 2 + z // 2) * 2 + core, lax.rem(z, 2) * 4 + x)

    def shifted(offsets, flip=0):
        c = {axis: lax.rem(me[axis] + offsets.get(axis, 0), 4) for axis in me}
        return device(c["x"], c["y"], c["z"], lax.rem(core + flip, 2))

    def offsets_over(axes):
        out = [{}]
        for axis in axes:
            out = [{**o, axis: i} for o in out for i in range(4)]
        far = lambda o: -sum((0, 1, 2, 1)[i] for i in o.values())
        return sorted([o for o in out if any(o.values())], key=far)

    plane, line = offsets_over("xy"), offsets_over("z")
    others = [{"y": i, "z": j} for i in (2, 1, 3, 0) for j in (2, 0) if i or j]
    sums = [(o, flip) for o in others for flip in (0, 1)] + [({}, 1)]
    tensor = [(d, lax.rem(t + i, 8)) for i in range(1, 8)]
    peers = [shifted(o) for o in plane + line]
    peers += [shifted(o, flip) for o, flip in sums if flip or (o["y"] and o["z"])]
    peers += [(d, lax.rem(zl + 1, 2) * 4 + lax.rem(x + i, 4)) for i in (1, 2, 3)]
    barrier = pltpu.get_barrier_semaphore()
    loads = [pltpu.make_async_copy(hid_hbm, hid, load_sem.at[0]),
             pltpu.make_async_copy(pg_hbm, pg, load_sem.at[1])]
    for load in loads:
        load.start()
    for peer in peers:
        pl.semaphore_signal(barrier, inc=1, device_id=peer, device_id_type=MESH)
    for load in loads:
        load.wait()
    grads = pg[...]
    high = grads.astype(BF16)
    out_buf[...] = high
    own_ref[t] = out_buf[t]
    flat_high = high.reshape(-1, high.shape[2])
    low = (grads.reshape(flat_high.shape) - flat_high.astype(F32)).astype(BF16)
    total = dot(hid[...], flat_high, TN) + dot(hid[...], low, TN)
    part[...] = total.astype(BF16).reshape(part.shape)
    pl.semaphore_wait(barrier, len(peers))

    def send(src, dst, sems, i, peer):
        copy = pltpu.make_async_remote_copy(
            src_ref=src, dst_ref=dst, send_sem=sems.at[0, i], recv_sem=sems.at[1, i],
            device_id=peer, device_id_type=MESH)
        copy.start()
        return copy

    scatter = []
    for i, (o, flip) in enumerate(sums):
        to = shifted(o, flip)
        scatter.append(send(part.at[to[0]], landed.at[i], sems_rs, i, to))
    back = [send(out_buf.at[to[1]], own_ref.at[t], sems_pg, i, to) for i, to in enumerate(tensor)]
    chunk = part[d].astype(F32)
    for i, copy in enumerate(scatter):
        copy.wait()
        chunk += landed[i].astype(F32)
    chunk = (chunk * (1.0 / SEQS)).astype(BF16)
    half = chunk.shape[1] // 2
    all_ref[0, core, z, y, x] = chunk[:, :half]
    all_ref[1, core, y, x, z] = chunk[:, half:]
    first = [send(all_ref.at[0, core, z, y, x], all_ref.at[0, core, z, y, x], sems_ag, i, shifted(o))
             for i, o in enumerate(plane)]
    first += [send(all_ref.at[1, core, y, x, z], all_ref.at[1, core, y, x, z], sems_ag, 15 + i, shifted(o))
              for i, o in enumerate(line)]
    for copy in first[15:]:
        copy.wait()
    wide = [send(all_ref.at[1, core, y, x], all_ref.at[1, core, y, x], sems_ag, 18 + i, shifted(o))
            for i, o in enumerate(plane)]
    for copy in first[:15]:
        copy.wait()
    deep = [send(all_ref.at[0, core, z], all_ref.at[0, core, z], sems_ag, 33 + i, shifted(o))
            for i, o in enumerate(line)]
    sibling = shifted({}, 1)
    passed = [send(all_ref.at[0, core, z], all_ref.at[0, core, z], sems_core, 0, sibling)]
    for o, copy in zip(line, deep):
        copy.wait()
        block = all_ref.at[0, core, lax.rem(z + 4 - o["z"], 4)]
        passed.append(send(block, block, sems_core, o["z"], sibling))
    for i in (2, 1, 3, 0):
        for o, copy in zip(plane, wide):
            if o["y"] == i:
                copy.wait()
        block = all_ref.at[1, core, lax.rem(y + 4 - i, 4)]
        passed.append(send(block, block, sems_core, 4 + i, sibling))
    for copy in passed + back:
        copy.wait()


def exchange(hidden, pgrads):
    n, plen, cols = pgrads.shape
    width = hidden.shape[1]
    rows = width // 16
    vmem = pl.BlockSpec(memory_space=pltpu.VMEM)
    return pl.pallas_call(
        exchange_kernel,
        out_shape=(jax.ShapeDtypeStruct((n, plen, cols), BF16),
                   jax.ShapeDtypeStruct((2, 2, 4, 4, 4, rows, cols // 2), BF16)),
        in_specs=[pl.BlockSpec(memory_space=pltpu.HBM)] * 2,
        out_specs=(vmem, vmem),
        scratch_shapes=[
            pltpu.VMEM(hidden.shape, BF16),
            pltpu.VMEM(pgrads.shape, F32),
            pltpu.VMEM((n, plen, cols), BF16),
            pltpu.VMEM((16, rows, cols), BF16),
            pltpu.VMEM((16, rows, cols), BF16),
            pltpu.SemaphoreType.DMA((2,)),
            pltpu.SemaphoreType.DMA((2, 8)),
            pltpu.SemaphoreType.DMA((2, 16)),
            pltpu.SemaphoreType.DMA((2, 36)),
            pltpu.SemaphoreType.DMA((2, 8)),
        ],
        compiler_params=pltpu.CompilerParams(collective_id=1, has_side_effects=True, vmem_limit_bytes=56 * 1024 * 1024),
        name="exchange",
    )(hidden, pgrads)


def finish_kernel(own_ref, first_ref, second_ref, prefix_grad_ref, weight_grad_ref):
    cols = own_ref.shape[2]
    half = cols // 2
    for j in range(own_ref.shape[0]):
        prefix_grad_ref[0, :, j * cols:(j + 1) * cols] = own_ref[j].astype(F32)
    ys, rows = first_ref.shape[3], first_ref.shape[5]
    for y in range(ys):
        for core in range(2):
            for z in range(4):
                r0 = ((y * 2 + z // 2) * 2 + core) * rows
                for x in range(4):
                    c0 = ((z % 2) * 4 + x) * cols
                    weight_grad_ref[r0:r0 + rows, c0:c0 + half] = first_ref[0, core, z, y, x].astype(F32)
                    weight_grad_ref[r0:r0 + rows, c0 + half:c0 + cols] = second_ref[0, core, y, x, z].astype(F32)


def finish(own, gathered, steps=2):
    n, plen, cols = own.shape
    rows = gathered.shape[5]
    ys = 4 // steps
    return pl.pallas_call(
        finish_kernel,
        grid=(steps,),
        out_shape=(jax.ShapeDtypeStruct((1, plen, n * cols), F32),
                   jax.ShapeDtypeStruct((16 * rows, n * cols), F32)),
        in_specs=[pl.BlockSpec((n // steps, plen, cols), lambda i: (i, 0, 0)),
                  pl.BlockSpec((1, 2, 4, ys, 4, rows, cols // 2), lambda i: (0, 0, 0, i, 0, 0, 0)),
                  pl.BlockSpec((1, 2, ys, 4, 4, rows, cols // 2), lambda i: (1, 0, i, 0, 0, 0, 0))],
        out_specs=(pl.BlockSpec((1, plen, n // steps * cols), lambda i: (0, 0, i)),
                   pl.BlockSpec((4 * ys * rows, n * cols), lambda i: (i, 0))),
        compiler_params=pltpu.CompilerParams(vmem_limit_bytes=56 * 1024 * 1024),
        name="widen",
    )(own, gathered, gathered)


def shards(tag_ids, tag_amounts, tag_table, position_table, prefix_weight,
           query_own, key_own, value_own, out_grad, seq_lengths):
    prefix, hidden = encode(tag_ids, tag_amounts, tag_table, position_table, prefix_weight)
    attn_out, pgrads = attention(seq_lengths, query_own, key_own, value_own, out_grad, prefix)
    prefix_grad, weight_grad = finish(*exchange(hidden, pgrads))
    return attn_out, prefix_grad, weight_grad


def solution(mesh):
    return jax.shard_map(
        shards,
        mesh=mesh,
        in_specs=(
            P(("dp", "tensor"), None),
            P(("dp", "tensor"), None),
            P(),
            P(),
            P(),
            P("dp", None, "tensor"),
            P("dp", None, "tensor"),
            P("dp", None, "tensor"),
            P("dp", None, "tensor"),
            P("dp"),
        ),
        out_specs=(P("dp", None, "tensor"), P(("dp", "tensor"), None, None), P()),
        check_vma=False,
    )
```

```python
import functools
import jax
import jax.numpy as jnp
from jax import lax
from jax.experimental import pallas as pl
from jax.experimental.pallas import tpu as pltpu
from jax.sharding import PartitionSpec as P

HD = 128
SEQS = 128
F32 = jnp.float32
BF16 = jnp.bfloat16
SCALE = 1.0 / HD**0.5
LOG2E = 1.4426950408889634
NT = (((1,), (1,)), ((), ()))
TN = (((0,), (0,)), ((), ()))
MESH = pl.DeviceIdType.MESH


def dot(a, b, dims=(((1,), (0,)), ((), ()))):
    return lax.dot_general(a, b, dims, preferred_element_type=F32)


def in_hbm(*arrays):
    return [pltpu.with_memory_space_constraint(a, pltpu.HBM) for a in arrays]


def hidden_of(mixture, table, pos):
    pooled = jnp.dot(mixture, table.astype(F32), precision=lax.Precision.HIGHEST, preferred_element_type=F32)
    pos = pos.astype(F32)
    return jnp.concatenate([jnp.tanh(pos + pooled[j:j + 1]) for j in range(mixture.shape[0])], 0).astype(BF16)


def attention_scratch(rows, width, plen):
    seg_w = width // HD * plen
    return [
        pltpu.VMEM((seg_w + rows, 2 * HD), BF16),
        pltpu.VMEM((seg_w, width), BF16),
        pltpu.VMEM((seg_w, width), BF16),
        pltpu.VMEM((rows, seg_w), BF16),
        pltpu.VMEM((rows, seg_w), BF16),
        pltpu.VMEM((rows, seg_w), F32),
    ]


def clear(vx, pkbd, pvbd):
    pkbd[...] = jnp.zeros_like(pkbd)
    pvbd[...] = jnp.zeros_like(pvbd)
    seg_w = pkbd.shape[0]
    vx[0:seg_w, HD:] = jnp.ones((seg_w, HD), BF16)


def place(length, prefix, v, vx, pkbd, pvbd):
    plen, seg_w, rows = prefix.shape[0], pkbd.shape[0], v.shape[0]
    pk, pv = prefix[:, :HD], prefix[:, HD:]
    for h in range(seg_w // plen):
        pkbd[h * plen:(h + 1) * plen, h * HD:(h + 1) * HD] = pk
        pvbd[h * plen:(h + 1) * plen, h * HD:(h + 1) * HD] = pv
        vx[h * plen:(h + 1) * plen, :HD] = pv
    live = lax.broadcasted_iota(jnp.int32, (rows, HD), 0) < length
    vx[seg_w:, :HD] = jnp.where(live, v.astype(F32), 0.0).astype(BF16)
    vx[seg_w:, HD:] = jnp.where(live, 1.0, 0.0).astype(BF16)


def row_delta(g, out, plen):
    heads = g.shape[1] // HD
    seg = lax.broadcasted_iota(jnp.int32, (g.shape[0], heads * plen), 1) // plen
    delta = None
    for h in range(heads):
        lanes = slice(h * HD, (h + 1) * HD)
        total = jnp.sum(g[:, lanes].astype(F32) * out[:, lanes].astype(F32), axis=1, keepdims=True)
        delta = jnp.broadcast_to(total, seg.shape) if h == 0 else jnp.where(seg == h, total, delta)
    return delta


def prefix_gradient(q_ref, g_ref, ds_scr, w_scr, plen):
    heads = q_ref.shape[1] // HD
    for half in range(heads // 2):
        lanes = slice(half * 2 * HD, (half + 1) * 2 * HD)
        dk = dot(ds_scr[...], q_ref[:, lanes], TN)
        dv = dot(w_scr[...], g_ref[:, lanes], TN)
        for i in range(2):
            h = half * 2 + i
            a = dk[h * plen:(h + 1) * plen, i * HD:(i + 1) * HD] * SCALE
            b = dv[h * plen:(h + 1) * plen, i * HD:(i + 1) * HD]
            if h:
                a, b = a + pa, b + pb
            pa, pb = a, b
    return jnp.concatenate([pa, pb], 1)


def attend_fast(length, q_ref, k_ref, g_ref, out_ref, plen, vx, pkbd, pvbd, ds_scr, w_scr, pp_scr,
                nr=128, groups=2, late=2):
    rows, width = q_ref.shape
    heads = width // HD
    seg_w = heads * plen
    per = heads // groups
    seg = lax.broadcasted_iota(jnp.int32, (nr, seg_w), 1) // plen
    causal = (lax.broadcasted_iota(jnp.int32, (per * nr, nr), 1)
              <= lax.broadcasted_iota(jnp.int32, (per * nr, nr), 0) % nr)
    c = SCALE * LOG2E

    def score_phase(r0):
        qr = q_ref[r0:r0 + nr]
        pp = jnp.exp2(dot(qr, pkbd[...], NT) * c)
        ppb = pp.astype(BF16)
        zero = jnp.zeros_like(ppb)
        ps = []
        for j in range(groups):
            hs = range(j * per, (j + 1) * per)
            q4 = jnp.concatenate([qr[:, h * HD:(h + 1) * HD] for h in hs], 0)
            parts = [jnp.concatenate([jnp.where(seg == h, ppb, zero) for h in hs], 0)]
            if r0:
                parts.append(jnp.exp2(dot(q4, k_ref[:r0], NT) * c).astype(BF16))
            diag = jnp.exp2(dot(q4, k_ref[r0:r0 + nr], NT) * c)
            parts.append(jnp.where(causal, diag, 0.0).astype(BF16))
            ps.append(jnp.concatenate(parts, 1))
        return pp, ps

    def value_phase(r0, pp, ps, bad):
        invs = []
        os = [dot(p, vx[:seg_w + r0 + nr]) for p in ps]
        for j, o in enumerate(os):
            sums = o[:, HD:]
            ok = (sums > 1e-25) & (sums < 1e25)
            bad = jnp.maximum(bad, jnp.max(jnp.where(ok, 0.0, 1.0).reshape(-1, 8, HD), axis=0))
            inv = 1.0 / sums
            o = (o[:, :HD] * inv).astype(BF16)
            for i in range(per):
                h = j * per + i
                invs.append(inv[i * nr:(i + 1) * nr])
                out_ref[r0:r0 + nr, h * HD:(h + 1) * HD] = o[i * nr:(i + 1) * nr]
        inv_seg = invs[0]
        for h in range(1, heads):
            inv_seg = jnp.where(seg == h, invs[h], inv_seg)
        alive = lax.broadcasted_iota(jnp.int32, (nr, seg_w), 0) + r0 < length
        probs = jnp.where(alive, pp * inv_seg, 0.0)
        w_scr[r0:r0 + nr] = probs.astype(BF16)
        pp_scr[r0:r0 + nr] = probs
        return bad

    bad = jnp.zeros((8, HD), F32)
    starts = list(range(0, rows, nr))
    state = score_phase(starts[0])
    for i, r0 in enumerate(starts):
        now = state
        if i + 1 < len(starts):
            state = score_phase(starts[i + 1])
        bad = value_phase(r0, *now, bad)
    step = rows // late
    for r0 in range(0, rows, step):
        g = g_ref[r0:r0 + step]
        delta = row_delta(g, out_ref[r0:r0 + step], plen)
        ds_scr[r0:r0 + step] = (pp_scr[r0:r0 + step] * (dot(g, pvbd[...], NT) - delta)).astype(BF16)
    return prefix_gradient(q_ref, g_ref, ds_scr, w_scr, plen), bad


def attend_exact(length, q_ref, k_ref, g_ref, out_ref, plen, vx, pkbd, pvbd, ds_scr, w_scr, pp_scr):
    nr = HD
    rows, width = q_ref.shape
    heads = width // HD
    seg_w = heads * plen
    seg = lax.broadcasted_iota(jnp.int32, (nr, seg_w), 1) // plen

    def block(r, carry):
        r0 = pl.multiple_of(r * nr, nr)
        here = pl.ds(r0, nr)
        sp_all = dot(q_ref[here], pkbd[...], NT) * SCALE
        row = lax.broadcasted_iota(jnp.int32, (nr, rows), 0) + r0
        col = lax.broadcasted_iota(jnp.int32, (nr, rows), 1)
        seen = (col <= row) & (col < length)
        pp_scr[here] = jnp.zeros((nr, seg_w), F32)

        def head(h, carry):
            lanes = pl.ds(pl.multiple_of(h * HD, HD), HD)
            s = jnp.where(seen, dot(q_ref[here, lanes], k_ref[...], NT) * SCALE, -1e30)
            sp = jnp.where(seg == h, sp_all, -1e30)
            m = jnp.maximum(jnp.max(s, axis=1, keepdims=True), jnp.max(sp, axis=1, keepdims=True))
            p = jnp.exp(s - m)
            p_pre = jnp.exp(sp - m)
            inv = 1.0 / (jnp.sum(p, axis=1, keepdims=True) + jnp.sum(p_pre, axis=1, keepdims=True))
            p_pre = p_pre * inv
            o = dot((p * inv).astype(BF16), vx[seg_w:, :HD]) + dot(p_pre.astype(BF16), vx[:seg_w, :HD])
            out_ref[here, lanes] = o.astype(BF16)
            pp_scr[here] += p_pre
            return carry

        lax.fori_loop(0, heads, head, 0)
        alive = lax.broadcasted_iota(jnp.int32, (nr, seg_w), 0) + r0 < length
        probs = jnp.where(alive, pp_scr[here], 0.0)
        w_scr[here] = probs.astype(BF16)
        g = g_ref[here]
        ds_scr[here] = (probs * (dot(g, pvbd[...], NT) - row_delta(g, out_ref[here], plen))).astype(BF16)
        return carry

    lax.fori_loop(0, rows // nr, block, 0)
    return prefix_gradient(q_ref, g_ref, ds_scr, w_scr, plen)


def encode_kernel(n, len_ref, ids_hbm, amt_hbm, table_hbm, pos_hbm, weight_hbm, q_hbm, k_hbm, v_hbm, g_hbm,
                  prefix_ref, hidden_ref, out_ref, pg_ref, bad_ref, me_ref,
                  ids_ref, amt_ref, table_ref, pos_ref, wbuf, q_ref, k_ref, v_ref, g_ref, mine, got,
                  send_sem, recv_sem, load_sem, *scratch):
    d, t = lax.axis_index("dp"), lax.axis_index("tensor")
    me_ref[0] = t
    cols = wbuf.shape[1]
    loads = [pltpu.make_async_copy(src, dst, load_sem.at[i]) for i, (src, dst) in enumerate((
        (ids_hbm, ids_ref), (amt_hbm, amt_ref), (table_hbm, table_ref), (pos_hbm, pos_ref),
        (weight_hbm.at[:, pl.ds(pl.multiple_of(t * cols, cols), cols)], wbuf),
        (q_hbm.at[t], q_ref), (k_hbm.at[t], k_ref), (v_hbm.at[t], v_ref), (g_hbm.at[t], g_ref)))]
    for load in loads:
        load.start()
    barrier = pltpu.get_barrier_semaphore()
    for i in range(1, n):
        pl.semaphore_signal(barrier, inc=1, device_id=(d, lax.rem(t + i, n)), device_id_type=MESH)
    loads[0].wait()
    loads[1].wait()
    tags = table_ref.shape[0]
    lane = lax.broadcasted_iota(jnp.int32, (1, tags), 1)
    ids, amounts = ids_ref[...], amt_ref[...]
    mix = jnp.zeros((1, tags), F32)
    for k in range(ids.shape[1]):
        mix += jnp.where(ids[:, k:k + 1] == lane, amounts[:, k:k + 1], 0.0)
    mix = mix / jnp.sum(amounts, axis=1, keepdims=True)
    mine[...] = jnp.broadcast_to(mix, mine.shape)
    got[t] = jnp.broadcast_to(mix, mine.shape)
    for load in loads[2:5]:
        load.wait()
    plen = pos_ref.shape[0]
    vx, pkbd, pvbd, ds_scr, w_scr, pp_scr = scratch
    length = len_ref[t]
    clear(vx, pkbd, pvbd)
    own = dot(hidden_of(mix, table_ref[...], pos_ref[...]), wbuf[...]).astype(BF16)
    pl.semaphore_wait(barrier, n - 1)
    copies = []
    for i in range(1, n):
        copy = pltpu.make_async_remote_copy(
            src_ref=mine, dst_ref=got.at[t], send_sem=send_sem.at[i], recv_sem=recv_sem.at[i],
            device_id=(d, lax.rem(t + i, n)), device_id_type=MESH)
        copy.start()
        copies.append(copy)
    for load in loads[5:]:
        load.wait()
    place(length, own, v_ref[...], vx, pkbd, pvbd)
    pg_ref[...], bad_ref[...] = attend_fast(length, q_ref, k_ref, g_ref, out_ref, plen, *scratch)
    for copy in copies:
        copy.wait()
    mixture = jnp.concatenate([got[j, 0:1] for j in range(n)], 0)
    hidden = hidden_of(mixture, table_ref[...], pos_ref[...])
    hidden_ref[...] = hidden
    prefix_ref[...] = dot(hidden, wbuf[...]).astype(BF16).reshape(prefix_ref.shape)


def encode(lengths, tag_ids, tag_amounts, tag_table, position_table, prefix_weight, q, k, v, g):
    n, rows, width = q.shape
    units, total = prefix_weight.shape
    plen = position_table.shape[0]
    cols = total // n
    vmem = pl.BlockSpec(memory_space=pltpu.VMEM)
    smem = pl.BlockSpec(memory_space=pltpu.SMEM)
    return pl.pallas_call(
        functools.partial(encode_kernel, n),
        out_shape=(pltpu.VMEM((n, plen, cols), BF16), pltpu.VMEM((n * plen, units), BF16),
                   pltpu.VMEM((rows, width), BF16), pltpu.VMEM((plen, cols), F32),
                   pltpu.VMEM((8, HD), F32), jax.ShapeDtypeStruct((1,), jnp.int32)),
        in_specs=[smem] + [pl.BlockSpec(memory_space=pltpu.HBM)] * 9,
        out_specs=(vmem,) * 5 + (smem,),
        scratch_shapes=[
            pltpu.VMEM(tag_ids.shape, jnp.int32),
            pltpu.VMEM(tag_amounts.shape, F32),
            pltpu.VMEM(tag_table.shape, BF16),
            pltpu.VMEM(position_table.shape, BF16),
            pltpu.VMEM((units, cols), BF16),
            pltpu.VMEM((rows, width), BF16),
            pltpu.VMEM((rows, HD), BF16),
            pltpu.VMEM((rows, HD), BF16),
            pltpu.VMEM((rows, width), BF16),
            pltpu.VMEM((8, tag_table.shape[0]), F32),
            pltpu.VMEM((n, 8, tag_table.shape[0]), F32),
            pltpu.SemaphoreType.DMA((n,)),
            pltpu.SemaphoreType.DMA((n,)),
            pltpu.SemaphoreType.DMA((9,)),
        ] + attention_scratch(rows, width, plen),
        compiler_params=pltpu.CompilerParams(
            collective_id=0, has_side_effects=True, vmem_limit_bytes=24 * 1024 * 1024),
        name="encode",
    )(*in_hbm(lengths, tag_ids, tag_amounts, tag_table, position_table, prefix_weight, q, k, v, g))


def attend_kernel(me_ref, len_ref, q_ref, k_ref, v_ref, g_ref, prefix_ref, own_out, own_pg, own_bad,
                  q_hbm, k_hbm, v_hbm, g_hbm, out_hbm, pg_ref,
                  outs, bad_scr, oq, ok, ov, og, out_sem, own_sem, *scratch):
    step, last = pl.program_id(0), pl.num_programs(0) - 1
    me = me_ref[0]
    here = lax.rem(me + 1 + step, last + 2)
    slot = lax.rem(step, 2)
    plen = prefix_ref.shape[1]
    vx, pkbd, pvbd = scratch[:3]
    q, k, g, out = q_ref.at[0], k_ref.at[0], g_ref.at[0], outs.at[slot]
    own_copy = pltpu.make_async_copy(own_out, out_hbm.at[me], own_sem.at[0])

    @pl.when(step == 0)
    def _():
        own_copy.start()
        clear(vx, pkbd, pvbd)

    @pl.when(step >= 2)
    def _():
        pltpu.make_async_copy(out, out_hbm.at[here], out_sem.at[slot]).wait()

    length = len_ref[here]
    place(length, prefix_ref[here], v_ref[0], vx, pkbd, pvbd)
    pg_ref[here], bad_scr[...] = attend_fast(length, q, k, g, out, plen, *scratch)

    @pl.when(jnp.max(bad_scr[...]) > 0.0)
    def _():
        pg_ref[here] = attend_exact(length, q, k, g, out, plen, *scratch)

    pltpu.make_async_copy(out, out_hbm.at[here], out_sem.at[slot]).start()

    @pl.when(step == last)
    def _():
        own_copy.wait()
        pg_ref[me] = own_pg[...]
        pltpu.make_async_copy(outs.at[1 - slot], out_hbm.at[here], out_sem.at[1 - slot]).wait()

        @pl.when(jnp.max(own_bad[...]) > 0.0)
        def _():
            loads = [pltpu.make_async_copy(src.at[me], dst, own_sem.at[i]) for i, (src, dst) in enumerate(
                ((q_hbm, oq), (k_hbm, ok), (v_hbm, ov), (g_hbm, og)))]
            for load in loads:
                load.start()
            for load in loads:
                load.wait()
            place(len_ref[me], prefix_ref[me], ov[...], vx, pkbd, pvbd)
            again = outs.at[1 - slot]
            pg_ref[me] = attend_exact(len_ref[me], oq, ok, og, again, plen, *scratch)
            store = pltpu.make_async_copy(again, out_hbm.at[me], own_sem.at[0])
            store.start()
            store.wait()

        pltpu.make_async_copy(out, out_hbm.at[here], out_sem.at[slot]).wait()


def attention(me, lengths, q, k, v, g, prefix, own_out, own_pg, own_bad):
    n, rows, width = q.shape
    plen, cols = prefix.shape[1:]
    spec = lambda shape: pl.BlockSpec((1,) + shape, lambda e, me: (lax.rem(me[0] + 1 + e, n), 0, 0))
    vmem = pl.BlockSpec(memory_space=pltpu.VMEM)
    hbm = pl.BlockSpec(memory_space=pltpu.HBM)
    tokens = in_hbm(q, k, v, g)
    return pl.pallas_call(
        attend_kernel,
        grid_spec=pltpu.PrefetchScalarGridSpec(
            num_scalar_prefetch=1,
            grid=(n - 1,),
            in_specs=[pl.BlockSpec(memory_space=pltpu.SMEM), spec((rows, width)), spec((rows, HD)),
                      spec((rows, HD)), spec((rows, width))] + [vmem] * 4 + [hbm] * 4,
            out_specs=(hbm, vmem),
            scratch_shapes=[
                pltpu.VMEM((2, rows, width), BF16),
                pltpu.VMEM((8, HD), F32),
                pltpu.VMEM((rows, width), BF16),
                pltpu.VMEM((rows, HD), BF16),
                pltpu.VMEM((rows, HD), BF16),
                pltpu.VMEM((rows, width), BF16),
                pltpu.SemaphoreType.DMA((2,)),
                pltpu.SemaphoreType.DMA((4,)),
            ] + attention_scratch(rows, width, plen),
        ),
        out_shape=(pltpu.HBM(q.shape, BF16), pltpu.VMEM((n, plen, cols), F32)),
        compiler_params=pltpu.CompilerParams(vmem_limit_bytes=40 * 1024 * 1024),
        name="attend",
    )(me, *in_hbm(lengths), *tokens, prefix, own_out, own_pg, own_bad, *tokens)


def exchange_kernel(hid, pg, own_ref, all_ref, out_buf, part, landed,
                    sems_pg, sems_rs, sems_ag, sems_core):
    d, t = lax.axis_index("dp"), lax.axis_index("tensor")
    y, zh, core = d // 4, lax.rem(d // 2, 2), lax.rem(d, 2)
    zl, x = t // 4, lax.rem(t, 4)
    z = zh * 2 + zl
    me = dict(x=x, y=y, z=z)

    def device(x, y, z, core):
        return ((y * 2 + z // 2) * 2 + core, lax.rem(z, 2) * 4 + x)

    def shifted(offsets, flip=0):
        c = {axis: lax.rem(me[axis] + offsets.get(axis, 0), 4) for axis in me}
        return device(c["x"], c["y"], c["z"], lax.rem(core + flip, 2))

    def offsets_over(axes):
        out = [{}]
        for axis in axes:
            out = [{**o, axis: i} for o in out for i in range(4)]
        far = lambda o: -sum((0, 1, 2, 1)[i] for i in o.values())
        return sorted([o for o in out if any(o.values())], key=far)

    plane, line = offsets_over("xy"), offsets_over("z")
    others = [{"y": i, "z": j} for i in (2, 1, 3, 0) for j in (2, 0) if i or j]
    sums = [(o, flip) for o in others for flip in (0, 1)] + [({}, 1)]
    tensor = [(d, lax.rem(t + i, 8)) for i in range(1, 8)]
    peers = [shifted(o) for o in plane + line]
    peers += [shifted(o, flip) for o, flip in sums if flip or (o["y"] and o["z"])]
    peers += [(d, lax.rem(zl + 1, 2) * 4 + lax.rem(x + i, 4)) for i in (1, 2, 3)]
    barrier = pltpu.get_barrier_semaphore()
    for peer in peers:
        pl.semaphore_signal(barrier, inc=1, device_id=peer, device_id_type=MESH)
    grads = pg[...]
    high = grads.astype(BF16)
    out_buf[...] = high
    own_ref[t] = out_buf[t]
    flat_high = high.reshape(-1, high.shape[2])
    low = (grads.reshape(flat_high.shape) - flat_high.astype(F32)).astype(BF16)
    total = dot(hid[...], flat_high, TN) + dot(hid[...], low, TN)
    part[...] = total.astype(BF16).reshape(part.shape)
    pl.semaphore_wait(barrier, len(peers))

    def send(src, dst, sems, i, peer):
        copy = pltpu.make_async_remote_copy(
            src_ref=src, dst_ref=dst, send_sem=sems.at[0, i], recv_sem=sems.at[1, i],
            device_id=peer, device_id_type=MESH)
        copy.start()
        return copy

    scatter = []
    for i, (o, flip) in enumerate(sums):
        to = shifted(o, flip)
        scatter.append(send(part.at[to[0]], landed.at[i], sems_rs, i, to))
    back = [send(out_buf.at[to[1]], own_ref.at[t], sems_pg, i, to) for i, to in enumerate(tensor)]
    chunk = part[d].astype(F32)
    for i, copy in enumerate(scatter):
        copy.wait()
        chunk += landed[i].astype(F32)
    chunk = (chunk * (1.0 / SEQS)).astype(BF16)
    half = chunk.shape[1] // 2
    all_ref[0, core, z, y, x] = chunk[:, :half]
    all_ref[1, core, y, x, z] = chunk[:, half:]
    first = [send(all_ref.at[0, core, z, y, x], all_ref.at[0, core, z, y, x], sems_ag, i, shifted(o))
             for i, o in enumerate(plane)]
    first += [send(all_ref.at[1, core, y, x, z], all_ref.at[1, core, y, x, z], sems_ag, 15 + i, shifted(o))
              for i, o in enumerate(line)]
    for copy in first[15:]:
        copy.wait()
    wide = [send(all_ref.at[1, core, y, x], all_ref.at[1, core, y, x], sems_ag, 18 + i, shifted(o))
            for i, o in enumerate(plane)]
    for copy in first[:15]:
        copy.wait()
    deep = [send(all_ref.at[0, core, z], all_ref.at[0, core, z], sems_ag, 33 + i, shifted(o))
            for i, o in enumerate(line)]
    sibling = shifted({}, 1)
    passed = [send(all_ref.at[0, core, z], all_ref.at[0, core, z], sems_core, 0, sibling)]
    for o, copy in zip(line, deep):
        copy.wait()
        block = all_ref.at[0, core, lax.rem(z + 4 - o["z"], 4)]
        passed.append(send(block, block, sems_core, o["z"], sibling))
    for i in (2, 1, 3, 0):
        for o, copy in zip(plane, wide):
            if o["y"] == i:
                copy.wait()
        block = all_ref.at[1, core, lax.rem(y + 4 - i, 4)]
        passed.append(send(block, block, sems_core, 4 + i, sibling))
    for copy in passed + back:
        copy.wait()


def exchange(hidden, pgrads):
    n, plen, cols = pgrads.shape
    width = hidden.shape[1]
    rows = width // 16
    vmem = pl.BlockSpec(memory_space=pltpu.VMEM)
    return pl.pallas_call(
        exchange_kernel,
        out_shape=(pltpu.VMEM((n, plen, cols), BF16), pltpu.VMEM((2, 2, 4, 4, 4, rows, cols // 2), BF16)),
        in_specs=[vmem] * 2,
        out_specs=(vmem, vmem),
        scratch_shapes=[
            pltpu.VMEM((n, plen, cols), BF16),
            pltpu.VMEM((16, rows, cols), BF16),
            pltpu.VMEM((16, rows, cols), BF16),
            pltpu.SemaphoreType.DMA((2, 8)),
            pltpu.SemaphoreType.DMA((2, 16)),
            pltpu.SemaphoreType.DMA((2, 36)),
            pltpu.SemaphoreType.DMA((2, 8)),
        ],
        compiler_params=pltpu.CompilerParams(collective_id=1, has_side_effects=True, vmem_limit_bytes=16 * 1024 * 1024),
        name="exchange",
    )(hidden, pgrads)


def finish_kernel(own_ref, first_ref, second_ref, prefix_grad_ref, weight_grad_ref):
    cols = own_ref.shape[2]
    half = cols // 2
    for j in range(own_ref.shape[0]):
        prefix_grad_ref[0, :, j * cols:(j + 1) * cols] = own_ref[j].astype(F32)
    ys, rows = first_ref.shape[3], first_ref.shape[5]
    for y in range(ys):
        for core in range(2):
            for z in range(4):
                r0 = ((y * 2 + z // 2) * 2 + core) * rows
                for x in range(4):
                    c0 = ((z % 2) * 4 + x) * cols
                    weight_grad_ref[r0:r0 + rows, c0:c0 + half] = first_ref[0, core, z, y, x].astype(F32)
                    weight_grad_ref[r0:r0 + rows, c0 + half:c0 + cols] = second_ref[0, core, y, x, z].astype(F32)


def finish(own, gathered, steps=2):
    n, plen, cols = own.shape
    rows = gathered.shape[5]
    ys = 4 // steps
    return pl.pallas_call(
        finish_kernel,
        grid=(steps,),
        out_shape=(pltpu.HBM((1, plen, n * cols), F32), pltpu.HBM((16 * rows, n * cols), F32)),
        in_specs=[pl.BlockSpec((n // steps, plen, cols), lambda i: (i, 0, 0)),
                  pl.BlockSpec((1, 2, 4, ys, 4, rows, cols // 2), lambda i: (0, 0, 0, i, 0, 0, 0)),
                  pl.BlockSpec((1, 2, ys, 4, 4, rows, cols // 2), lambda i: (1, 0, i, 0, 0, 0, 0))],
        out_specs=(pl.BlockSpec((1, plen, n // steps * cols), lambda i: (0, 0, i)),
                   pl.BlockSpec((4 * ys * rows, n * cols), lambda i: (i, 0))),
        compiler_params=pltpu.CompilerParams(vmem_limit_bytes=24 * 1024 * 1024),
        name="widen",
    )(own, gathered, gathered)


def shards(tag_ids, tag_amounts, tag_table, position_table, prefix_weight,
           query_own, key_own, value_own, out_grad, seq_lengths):
    tokens = (query_own, key_own, value_own, out_grad)
    prefix, hidden, own_out, own_pg, own_bad, me = encode(
        seq_lengths, tag_ids, tag_amounts, tag_table, position_table, prefix_weight, *tokens)
    attn_out, pgrads = attention(me, seq_lengths, *tokens, prefix, own_out, own_pg, own_bad)
    prefix_grad, weight_grad = finish(*exchange(hidden, pgrads))
    return attn_out, prefix_grad, weight_grad


def solution(mesh):
    return jax.shard_map(
        shards,
        mesh=mesh,
        in_specs=(
            P(("dp", "tensor"), None),
            P(("dp", "tensor"), None),
            P(),
            P(),
            P(),
            P("dp", None, "tensor"),
            P("dp", None, "tensor"),
            P("dp", None, "tensor"),
            P("dp", None, "tensor"),
            P("dp"),
        ),
        out_specs=(P("dp", None, "tensor"), P(("dp", "tensor"), None, None), P()),
        check_vma=False,
    )
```

```python
import functools
import jax
import jax.numpy as jnp
from jax import lax
from jax.experimental import pallas as pl
from jax.experimental.pallas import tpu as pltpu
from jax.sharding import PartitionSpec as P

HD = 128
SEQS = 128
F32 = jnp.float32
BF16 = jnp.bfloat16
SCALE = 1.0 / HD**0.5
LOG2E = 1.4426950408889634
NT = (((1,), (1,)), ((), ()))
TN = (((0,), (0,)), ((), ()))
MESH = pl.DeviceIdType.MESH


def dot(a, b, dims=(((1,), (0,)), ((), ()))):
    return lax.dot_general(a, b, dims, preferred_element_type=F32)


def in_hbm(*arrays):
    return [pltpu.with_memory_space_constraint(a, pltpu.HBM) for a in arrays]


def hidden_of(mixture, table, pos):
    pooled = jnp.dot(mixture, table.astype(F32), precision=lax.Precision.HIGHEST, preferred_element_type=F32)
    pos = pos.astype(F32)
    return jnp.concatenate([jnp.tanh(pos + pooled[j:j + 1]) for j in range(mixture.shape[0])], 0).astype(BF16)


def attention_scratch(rows, width, plen, sets=()):
    seg_w = width // HD * plen
    return [
        pltpu.VMEM((seg_w + rows, 2 * HD), BF16),
        pltpu.VMEM((seg_w, width), BF16),
        pltpu.VMEM((seg_w, width), BF16),
        pltpu.VMEM((*sets, rows, seg_w), BF16),
        pltpu.VMEM((*sets, rows, seg_w), BF16),
        pltpu.VMEM((rows, seg_w), F32),
    ]


def clear(vx, pkbd, pvbd):
    pkbd[...] = jnp.zeros_like(pkbd)
    pvbd[...] = jnp.zeros_like(pvbd)
    seg_w = pkbd.shape[0]
    vx[0:seg_w, HD:] = jnp.ones((seg_w, HD), BF16)


def place(length, prefix, v, vx, pkbd, pvbd):
    plen, seg_w, rows = prefix.shape[0], pkbd.shape[0], v.shape[0]
    pk, pv = prefix[:, :HD], prefix[:, HD:]
    for h in range(seg_w // plen):
        pkbd[h * plen:(h + 1) * plen, h * HD:(h + 1) * HD] = pk
        pvbd[h * plen:(h + 1) * plen, h * HD:(h + 1) * HD] = pv
        vx[h * plen:(h + 1) * plen, :HD] = pv
    live = lax.broadcasted_iota(jnp.int32, (rows, HD), 0) < length
    vx[seg_w:, :HD] = jnp.where(live, v.astype(F32), 0.0).astype(BF16)
    vx[seg_w:, HD:] = jnp.where(live, 1.0, 0.0).astype(BF16)


def row_delta(g, out, plen):
    heads = g.shape[1] // HD
    seg = lax.broadcasted_iota(jnp.int32, (g.shape[0], heads * plen), 1) // plen
    delta = None
    for h in range(heads):
        lanes = slice(h * HD, (h + 1) * HD)
        total = jnp.sum(g[:, lanes].astype(F32) * out[:, lanes].astype(F32), axis=1, keepdims=True)
        delta = jnp.broadcast_to(total, seg.shape) if h == 0 else jnp.where(seg == h, total, delta)
    return delta


def prefix_gradient(q_ref, g_ref, ds_scr, w_scr, plen):
    heads = q_ref.shape[1] // HD
    for half in range(heads // 2):
        lanes = slice(half * 2 * HD, (half + 1) * 2 * HD)
        dk = dot(ds_scr[...], q_ref[:, lanes], TN)
        dv = dot(w_scr[...], g_ref[:, lanes], TN)
        for i in range(2):
            h = half * 2 + i
            a = dk[h * plen:(h + 1) * plen, i * HD:(i + 1) * HD] * SCALE
            b = dv[h * plen:(h + 1) * plen, i * HD:(i + 1) * HD]
            if h:
                a, b = a + pa, b + pb
            pa, pb = a, b
    return jnp.concatenate([pa, pb], 1)


def attend_fast(length, q_ref, k_ref, g_ref, out_ref, plen, vx, pkbd, pvbd, ds_scr, w_scr, pp_scr,
                beside=None, nr=128, groups=2, late=2):
    rows, width = q_ref.shape
    heads = width // HD
    seg_w = heads * plen
    per = heads // groups
    seg = lax.broadcasted_iota(jnp.int32, (nr, seg_w), 1) // plen
    causal = (lax.broadcasted_iota(jnp.int32, (per * nr, nr), 1)
              <= lax.broadcasted_iota(jnp.int32, (per * nr, nr), 0) % nr)
    c = SCALE * LOG2E

    def score_phase(r0):
        qr = q_ref[r0:r0 + nr]
        pp = jnp.exp2(dot(qr, pkbd[...], NT) * c)
        ppb = pp.astype(BF16)
        zero = jnp.zeros_like(ppb)
        ps = []
        for j in range(groups):
            hs = range(j * per, (j + 1) * per)
            q4 = jnp.concatenate([qr[:, h * HD:(h + 1) * HD] for h in hs], 0)
            parts = [jnp.concatenate([jnp.where(seg == h, ppb, zero) for h in hs], 0)]
            if r0:
                parts.append(jnp.exp2(dot(q4, k_ref[:r0], NT) * c).astype(BF16))
            diag = jnp.exp2(dot(q4, k_ref[r0:r0 + nr], NT) * c)
            parts.append(jnp.where(causal, diag, 0.0).astype(BF16))
            ps.append(jnp.concatenate(parts, 1))
        return pp, ps

    def value_phase(r0, pp, ps, bad):
        invs = []
        os = [dot(p, vx[:seg_w + r0 + nr]) for p in ps]
        for j, o in enumerate(os):
            sums = o[:, HD:]
            ok = (sums > 1e-25) & (sums < 1e25)
            bad = jnp.maximum(bad, jnp.max(jnp.where(ok, 0.0, 1.0).reshape(-1, 8, HD), axis=0))
            inv = 1.0 / sums
            o = (o[:, :HD] * inv).astype(BF16)
            for i in range(per):
                h = j * per + i
                invs.append(inv[i * nr:(i + 1) * nr])
                out_ref[r0:r0 + nr, h * HD:(h + 1) * HD] = o[i * nr:(i + 1) * nr]
        inv_seg = invs[0]
        for h in range(1, heads):
            inv_seg = jnp.where(seg == h, invs[h], inv_seg)
        alive = lax.broadcasted_iota(jnp.int32, (nr, seg_w), 0) + r0 < length
        probs = jnp.where(alive, pp * inv_seg, 0.0)
        w_scr[r0:r0 + nr] = probs.astype(BF16)
        pp_scr[r0:r0 + nr] = probs
        return bad

    bad = jnp.zeros((8, HD), F32)
    starts = list(range(0, rows, nr))
    state = score_phase(starts[0])
    if beside is not None:
        beside()
    for i, r0 in enumerate(starts):
        now = state
        if i + 1 < len(starts):
            state = score_phase(starts[i + 1])
        bad = value_phase(r0, *now, bad)
    step = rows // late
    for r0 in range(0, rows, step):
        g = g_ref[r0:r0 + step]
        delta = row_delta(g, out_ref[r0:r0 + step], plen)
        ds_scr[r0:r0 + step] = (pp_scr[r0:r0 + step] * (dot(g, pvbd[...], NT) - delta)).astype(BF16)
    return bad


def attend_exact(length, q_ref, k_ref, g_ref, out_ref, plen, vx, pkbd, pvbd, ds_scr, w_scr, pp_scr):
    nr = HD
    rows, width = q_ref.shape
    heads = width // HD
    seg_w = heads * plen
    seg = lax.broadcasted_iota(jnp.int32, (nr, seg_w), 1) // plen

    def block(r, carry):
        r0 = pl.multiple_of(r * nr, nr)
        here = pl.ds(r0, nr)
        sp_all = dot(q_ref[here], pkbd[...], NT) * SCALE
        row = lax.broadcasted_iota(jnp.int32, (nr, rows), 0) + r0
        col = lax.broadcasted_iota(jnp.int32, (nr, rows), 1)
        seen = (col <= row) & (col < length)
        pp_scr[here] = jnp.zeros((nr, seg_w), F32)

        def head(h, carry):
            lanes = pl.ds(pl.multiple_of(h * HD, HD), HD)
            s = jnp.where(seen, dot(q_ref[here, lanes], k_ref[...], NT) * SCALE, -1e30)
            sp = jnp.where(seg == h, sp_all, -1e30)
            m = jnp.maximum(jnp.max(s, axis=1, keepdims=True), jnp.max(sp, axis=1, keepdims=True))
            p = jnp.exp(s - m)
            p_pre = jnp.exp(sp - m)
            inv = 1.0 / (jnp.sum(p, axis=1, keepdims=True) + jnp.sum(p_pre, axis=1, keepdims=True))
            p_pre = p_pre * inv
            o = dot((p * inv).astype(BF16), vx[seg_w:, :HD]) + dot(p_pre.astype(BF16), vx[:seg_w, :HD])
            out_ref[here, lanes] = o.astype(BF16)
            pp_scr[here] += p_pre
            return carry

        lax.fori_loop(0, heads, head, 0)
        alive = lax.broadcasted_iota(jnp.int32, (nr, seg_w), 0) + r0 < length
        probs = jnp.where(alive, pp_scr[here], 0.0)
        w_scr[here] = probs.astype(BF16)
        g = g_ref[here]
        ds_scr[here] = (probs * (dot(g, pvbd[...], NT) - row_delta(g, out_ref[here], plen))).astype(BF16)
        return carry

    lax.fori_loop(0, rows // nr, block, 0)


def encode_kernel(n, len_ref, ids_hbm, amt_hbm, table_hbm, pos_hbm, weight_hbm, q_hbm, k_hbm, v_hbm, g_hbm,
                  prefix_ref, hidden_ref, out_ref, pg_ref, bad_ref, nq, nk, nv, ng, me_ref,
                  ids_ref, amt_ref, table_ref, pos_ref, wbuf, q_ref, k_ref, v_ref, g_ref, mine, got,
                  send_sem, recv_sem, load_sem, *scratch):
    d, t = lax.axis_index("dp"), lax.axis_index("tensor")
    me_ref[0] = t
    cols = wbuf.shape[1]
    loads = [pltpu.make_async_copy(src, dst, load_sem.at[i]) for i, (src, dst) in enumerate((
        (ids_hbm, ids_ref), (amt_hbm, amt_ref), (table_hbm, table_ref), (pos_hbm, pos_ref),
        (weight_hbm.at[:, pl.ds(pl.multiple_of(t * cols, cols), cols)], wbuf),
        (q_hbm.at[t], q_ref), (k_hbm.at[t], k_ref), (v_hbm.at[t], v_ref), (g_hbm.at[t], g_ref)))]
    after = lax.rem(t + 1, n)
    ahead = [pltpu.make_async_copy(src.at[after], dst, load_sem.at[9 + i]) for i, (src, dst) in enumerate((
        (q_hbm, nq.at[0]), (k_hbm, nk.at[0]), (v_hbm, nv.at[0]), (g_hbm, ng.at[0])))]
    for load in loads:
        load.start()
    barrier = pltpu.get_barrier_semaphore()
    line = n // 2
    peers = [(d, lax.rem(t // line + a, 2) * line + lax.rem(t + b, line))
             for a, b in ((1, 2), (1, 1), (1, 3), (0, 2), (1, 0), (0, 1), (0, 3))]
    for peer in peers:
        pl.semaphore_signal(barrier, inc=1, device_id=peer, device_id_type=MESH)
    loads[0].wait()
    loads[1].wait()
    tags = table_ref.shape[0]
    lane = lax.broadcasted_iota(jnp.int32, (1, tags), 1)
    ids, amounts = ids_ref[...], amt_ref[...]
    mix = jnp.zeros((1, tags), F32)
    for k in range(ids.shape[1]):
        mix += jnp.where(ids[:, k:k + 1] == lane, amounts[:, k:k + 1], 0.0)
    mix = mix / jnp.sum(amounts, axis=1, keepdims=True)
    mine[...] = jnp.broadcast_to(mix, mine.shape)
    got[t] = jnp.broadcast_to(mix, mine.shape)
    for load in loads[2:5]:
        load.wait()
    plen = pos_ref.shape[0]
    vx, pkbd, pvbd, ds_scr, w_scr, pp_scr = scratch
    length = len_ref[t]
    clear(vx, pkbd, pvbd)
    own = dot(hidden_of(mix, table_ref[...], pos_ref[...]), wbuf[...]).astype(BF16)
    pl.semaphore_wait(barrier, n - 1)
    copies = []
    for i, peer in enumerate(peers):
        copy = pltpu.make_async_remote_copy(
            src_ref=mine, dst_ref=got.at[t], send_sem=send_sem.at[i], recv_sem=recv_sem.at[i],
            device_id=peer, device_id_type=MESH)
        copy.start()
        copies.append(copy)
    for load in loads[5:]:
        load.wait()
    for load in ahead:
        load.start()
    place(length, own, v_ref[...], vx, pkbd, pvbd)
    bad_ref[...] = attend_fast(length, q_ref, k_ref, g_ref, out_ref, plen, *scratch)
    pg_ref[...] = prefix_gradient(q_ref, g_ref, ds_scr, w_scr, plen)
    for copy in copies:
        copy.wait()
    mixture = jnp.concatenate([got[j, 0:1] for j in range(n)], 0)
    hidden = hidden_of(mixture, table_ref[...], pos_ref[...])
    hidden_ref[...] = hidden
    prefix_ref[...] = dot(hidden, wbuf[...]).astype(BF16).reshape(prefix_ref.shape)
    for load in ahead:
        load.wait()


def encode(lengths, tag_ids, tag_amounts, tag_table, position_table, prefix_weight, q, k, v, g):
    n, rows, width = q.shape
    units, total = prefix_weight.shape
    plen = position_table.shape[0]
    cols = total // n
    vmem = pl.BlockSpec(memory_space=pltpu.VMEM)
    smem = pl.BlockSpec(memory_space=pltpu.SMEM)
    return pl.pallas_call(
        functools.partial(encode_kernel, n),
        out_shape=(pltpu.VMEM((n, plen, cols), BF16), pltpu.VMEM((n * plen, units), BF16),
                   pltpu.VMEM((rows, width), BF16), pltpu.VMEM((plen, cols), F32),
                   pltpu.VMEM((8, HD), F32),
                   pltpu.VMEM((3, rows, width), BF16), pltpu.VMEM((3, rows, HD), BF16),
                   pltpu.VMEM((3, rows, HD), BF16), pltpu.VMEM((3, rows, width), BF16),
                   jax.ShapeDtypeStruct((1,), jnp.int32)),
        in_specs=[smem] + [pl.BlockSpec(memory_space=pltpu.HBM)] * 9,
        out_specs=(vmem,) * 9 + (smem,),
        scratch_shapes=[
            pltpu.VMEM(tag_ids.shape, jnp.int32),
            pltpu.VMEM(tag_amounts.shape, F32),
            pltpu.VMEM(tag_table.shape, BF16),
            pltpu.VMEM(position_table.shape, BF16),
            pltpu.VMEM((units, cols), BF16),
            pltpu.VMEM((rows, width), BF16),
            pltpu.VMEM((rows, HD), BF16),
            pltpu.VMEM((rows, HD), BF16),
            pltpu.VMEM((rows, width), BF16),
            pltpu.VMEM((8, tag_table.shape[0]), F32),
            pltpu.VMEM((n, 8, tag_table.shape[0]), F32),
            pltpu.SemaphoreType.DMA((n,)),
            pltpu.SemaphoreType.DMA((n,)),
            pltpu.SemaphoreType.DMA((13,)),
        ] + attention_scratch(rows, width, plen),
        compiler_params=pltpu.CompilerParams(
            collective_id=0, has_side_effects=True, vmem_limit_bytes=24 * 1024 * 1024),
        name="encode",
    )(*in_hbm(lengths, tag_ids, tag_amounts, tag_table, position_table, prefix_weight, q, k, v, g))


def attend_kernel(me_ref, len_ref, prefix_ref, own_out, own_pg, own_bad, _q, _k, _v, _g,
                  q_hbm, k_hbm, v_hbm, g_hbm, out_hbm, pg_ref, qs, ks, vs, gs,
                  outs, bad_scr, rq, rk, rv, rg, out_sem, in_sem, own_sem, redo_sem,
                  vx, pkbd, pvbd, ds_scr, w_scr, pp_scr):
    step, last = pl.program_id(0), pl.num_programs(0) - 1
    me = me_ref[0]
    here = lax.rem(me + 1 + step, last + 2)
    before = lax.rem(me + step, last + 2)
    slot, even = lax.rem(step, 3), lax.rem(step, 2)
    gone = lax.rem(step + 2, 3)
    plen = prefix_ref.shape[1]
    out = outs.at[even]
    own_copy = pltpu.make_async_copy(own_out, out_hbm.at[me], own_sem)

    def loads(example, into):
        return [pltpu.make_async_copy(src.at[example], dst.at[into], in_sem.at[into, i])
                for i, (src, dst) in enumerate(((q_hbm, qs), (k_hbm, ks), (v_hbm, vs), (g_hbm, gs)))]

    def store(into):
        return pltpu.make_async_copy(outs.at[into], out_hbm.at[here], out_sem.at[into])

    @pl.when(step == 0)
    def _():
        own_copy.start()
        clear(vx, pkbd, pvbd)

    @pl.when(step > 0)
    def _():
        for load in loads(here, slot):
            load.wait()

    @pl.when(step < last)
    def _():
        for load in loads(lax.rem(here + 1, last + 2), lax.rem(step + 1, 3)):
            load.start()

    @pl.when(step >= 2)
    def _():
        store(even).wait()

    def previous():
        pg_ref[before] = prefix_gradient(qs.at[gone], gs.at[gone], ds_scr.at[1 - even], w_scr.at[1 - even], plen)

    length = len_ref[here]
    place(length, prefix_ref[here], vs[slot], vx, pkbd, pvbd)
    scratch = (vx, pkbd, pvbd, ds_scr.at[even], w_scr.at[even], pp_scr)
    bad_scr[...] = attend_fast(length, qs.at[slot], ks.at[slot], gs.at[slot], out, plen, *scratch, beside=previous)

    @pl.when(jnp.max(bad_scr[...]) > 0.0)
    def _():
        attend_exact(length, qs.at[slot], ks.at[slot], gs.at[slot], out, plen, *scratch)

    store(even).start()

    @pl.when(step == last)
    def _():
        own_copy.wait()
        pg_ref[here] = prefix_gradient(qs.at[slot], gs.at[slot], ds_scr.at[even], w_scr.at[even], plen)
        pg_ref[me] = own_pg[...]
        store(1 - even).wait()

        @pl.when(jnp.max(own_bad[...]) > 0.0)
        def _():
            copies = [pltpu.make_async_copy(src.at[me], dst, redo_sem.at[i]) for i, (src, dst) in enumerate(
                ((q_hbm, rq), (k_hbm, rk), (v_hbm, rv), (g_hbm, rg)))]
            for copy in copies:
                copy.start()
            for copy in copies:
                copy.wait()
            place(len_ref[me], prefix_ref[me], rv[...], vx, pkbd, pvbd)
            attend_exact(len_ref[me], rq, rk, rg, outs.at[1 - even], plen, *scratch)
            pg_ref[me] = prefix_gradient(rq, rg, ds_scr.at[even], w_scr.at[even], plen)
            again = pltpu.make_async_copy(outs.at[1 - even], out_hbm.at[me], own_sem)
            again.start()
            again.wait()

        store(even).wait()


def attention(me, lengths, q, k, v, g, prefix, own_out, own_pg, own_bad, ahead):
    n, rows, width = q.shape
    plen, cols = prefix.shape[1:]
    smem = pl.BlockSpec(memory_space=pltpu.SMEM)
    vmem = pl.BlockSpec(memory_space=pltpu.VMEM)
    hbm = pl.BlockSpec(memory_space=pltpu.HBM)
    wide, narrow = (rows, width), (rows, HD)
    return pl.pallas_call(
        attend_kernel,
        grid=(n - 1,),
        in_specs=[smem, smem] + [vmem] * 8 + [hbm] * 4,
        out_specs=(hbm,) + (vmem,) * 5,
        scratch_shapes=[
            pltpu.VMEM((2, *wide), BF16),
            pltpu.VMEM((8, HD), F32),
            pltpu.VMEM(wide, BF16),
            pltpu.VMEM(narrow, BF16),
            pltpu.VMEM(narrow, BF16),
            pltpu.VMEM(wide, BF16),
            pltpu.SemaphoreType.DMA((2,)),
            pltpu.SemaphoreType.DMA((3, 4)),
            pltpu.SemaphoreType.DMA,
            pltpu.SemaphoreType.DMA((4,)),
        ] + attention_scratch(rows, width, plen, (2,)),
        out_shape=(pltpu.HBM(q.shape, BF16), pltpu.VMEM((n, plen, cols), F32),
                   *(pltpu.VMEM(buf.shape, BF16) for buf in ahead)),
        input_output_aliases={6 + i: 2 + i for i in range(4)},
        compiler_params=pltpu.CompilerParams(vmem_limit_bytes=40 * 1024 * 1024),
        name="attend",
    )(me, *in_hbm(lengths), prefix, own_out, own_pg, own_bad, *ahead, *in_hbm(q, k, v, g))


def exchange_kernel(hid, pg, own_ref, all_ref, out_buf, part, landed,
                    sems_pg, sems_rs, sems_ag, sems_core):
    d, t = lax.axis_index("dp"), lax.axis_index("tensor")
    y, zh, core = d // 4, lax.rem(d // 2, 2), lax.rem(d, 2)
    zl, x = t // 4, lax.rem(t, 4)
    z = zh * 2 + zl
    me = dict(x=x, y=y, z=z)

    def device(x, y, z, core):
        return ((y * 2 + z // 2) * 2 + core, lax.rem(z, 2) * 4 + x)

    def shifted(offsets, flip=0):
        c = {axis: lax.rem(me[axis] + offsets.get(axis, 0), 4) for axis in me}
        return device(c["x"], c["y"], c["z"], lax.rem(core + flip, 2))

    far = lambda o: -sum((0, 1, 2, 1)[i] for i in o.values())

    def offsets_over(axes):
        out = [{}]
        for axis in axes:
            out = [{**o, axis: i} for o in out for i in range(4)]
        return sorted([o for o in out if any(o.values())], key=far)

    plane, line = offsets_over("xy"), offsets_over("z")
    others = [{"y": i, "z": j} for i in (2, 1, 3, 0) for j in (2, 0) if i or j]
    sums = [(o, flip) for o in others for flip in (0, 1)] + [({}, 1)]
    tensor = [(d, lax.rem(t + i, 8)) for i in range(1, 8)]
    peers = [(far(o), shifted(o)) for o in plane + line]
    peers += [(far(o), shifted(o, flip)) for o, flip in sums if flip or (o["y"] and o["z"])]
    peers += [(-1 - (0, 1, 2, 1)[i], (d, lax.rem(zl + 1, 2) * 4 + lax.rem(x + i, 4))) for i in (1, 2, 3)]
    peers = [peer for _, peer in sorted(peers, key=lambda item: item[0])]
    barrier = pltpu.get_barrier_semaphore()
    for peer in peers:
        pl.semaphore_signal(barrier, inc=1, device_id=peer, device_id_type=MESH)
    grads = pg[...]
    high = grads.astype(BF16)
    out_buf[...] = high
    own_ref[t] = out_buf[t]
    flat_high = high.reshape(-1, high.shape[2])
    low = (grads.reshape(flat_high.shape) - flat_high.astype(F32)).astype(BF16)
    total = dot(hid[...], flat_high, TN) + dot(hid[...], low, TN)
    part[...] = total.astype(BF16).reshape(part.shape)
    pl.semaphore_wait(barrier, len(peers))

    def send(src, dst, sems, i, peer):
        copy = pltpu.make_async_remote_copy(
            src_ref=src, dst_ref=dst, send_sem=sems.at[0, i], recv_sem=sems.at[1, i],
            device_id=peer, device_id_type=MESH)
        copy.start()
        return copy

    scatter = []
    for i, (o, flip) in enumerate(sums):
        to = shifted(o, flip)
        scatter.append(send(part.at[to[0]], landed.at[i], sems_rs, i, to))
    back = [send(out_buf.at[to[1]], own_ref.at[t], sems_pg, i, to) for i, to in enumerate(tensor)]
    chunk = part[d].astype(F32)
    for i, copy in enumerate(scatter):
        copy.wait()
        chunk += landed[i].astype(F32)
    chunk = (chunk * (1.0 / SEQS)).astype(BF16)
    half = chunk.shape[1] // 2
    all_ref[0, core, z, y, x] = chunk[:, :half]
    all_ref[1, core, y, x, z] = chunk[:, half:]
    early = [send(all_ref.at[1, core, y, x, z], all_ref.at[1, core, y, x, z], sems_ag, i, shifted(o))
             for i, o in enumerate(line)]
    first = [send(all_ref.at[0, core, z, y, x], all_ref.at[0, core, z, y, x], sems_ag, 3 + i, shifted(o))
             for i, o in enumerate(plane)]
    for copy in early:
        copy.wait()
    wide = [send(all_ref.at[1, core, y, x], all_ref.at[1, core, y, x], sems_ag, 18 + i, shifted(o))
            for i, o in enumerate(plane)]
    for copy in first:
        copy.wait()
    deep = [send(all_ref.at[0, core, z], all_ref.at[0, core, z], sems_ag, 33 + i, shifted(o))
            for i, o in enumerate(line)]
    sibling = shifted({}, 1)
    passed = [send(all_ref.at[0, core, z], all_ref.at[0, core, z], sems_core, 0, sibling)]
    for o, copy in zip(line, deep):
        copy.wait()
        block = all_ref.at[0, core, lax.rem(z + 4 - o["z"], 4)]
        passed.append(send(block, block, sems_core, o["z"], sibling))
    for i in (2, 1, 3, 0):
        for o, copy in zip(plane, wide):
            if o["y"] == i:
                copy.wait()
        block = all_ref.at[1, core, lax.rem(y + 4 - i, 4)]
        passed.append(send(block, block, sems_core, 4 + i, sibling))
    for copy in passed + back:
        copy.wait()


def exchange(hidden, pgrads):
    n, plen, cols = pgrads.shape
    width = hidden.shape[1]
    rows = width // 16
    vmem = pl.BlockSpec(memory_space=pltpu.VMEM)
    return pl.pallas_call(
        exchange_kernel,
        out_shape=(pltpu.VMEM((n, plen, cols), BF16), pltpu.VMEM((2, 2, 4, 4, 4, rows, cols // 2), BF16)),
        in_specs=[vmem] * 2,
        out_specs=(vmem, vmem),
        scratch_shapes=[
            pltpu.VMEM((n, plen, cols), BF16),
            pltpu.VMEM((16, rows, cols), BF16),
            pltpu.VMEM((16, rows, cols), BF16),
            pltpu.SemaphoreType.DMA((2, 8)),
            pltpu.SemaphoreType.DMA((2, 16)),
            pltpu.SemaphoreType.DMA((2, 36)),
            pltpu.SemaphoreType.DMA((2, 8)),
        ],
        compiler_params=pltpu.CompilerParams(collective_id=1, has_side_effects=True, vmem_limit_bytes=16 * 1024 * 1024),
        name="exchange",
    )(hidden, pgrads)


def finish_kernel(own_ref, first_ref, second_ref, prefix_grad_ref, weight_grad_ref):
    cols = own_ref.shape[2]
    half = cols // 2
    for j in range(own_ref.shape[0]):
        prefix_grad_ref[0, :, j * cols:(j + 1) * cols] = own_ref[j].astype(F32)
    ys, rows = first_ref.shape[3], first_ref.shape[5]
    for y in range(ys):
        for core in range(2):
            for z in range(4):
                r0 = ((y * 2 + z // 2) * 2 + core) * rows
                for x in range(4):
                    c0 = ((z % 2) * 4 + x) * cols
                    weight_grad_ref[r0:r0 + rows, c0:c0 + half] = first_ref[0, core, z, y, x].astype(F32)
                    weight_grad_ref[r0:r0 + rows, c0 + half:c0 + cols] = second_ref[0, core, y, x, z].astype(F32)


def finish(own, gathered, steps=2):
    n, plen, cols = own.shape
    rows = gathered.shape[5]
    ys = 4 // steps
    return pl.pallas_call(
        finish_kernel,
        grid=(steps,),
        out_shape=(pltpu.HBM((1, plen, n * cols), F32), pltpu.HBM((16 * rows, n * cols), F32)),
        in_specs=[pl.BlockSpec((n // steps, plen, cols), lambda i: (i, 0, 0)),
                  pl.BlockSpec((1, 2, 4, ys, 4, rows, cols // 2), lambda i: (0, 0, 0, i, 0, 0, 0)),
                  pl.BlockSpec((1, 2, ys, 4, 4, rows, cols // 2), lambda i: (1, 0, i, 0, 0, 0, 0))],
        out_specs=(pl.BlockSpec((1, plen, n // steps * cols), lambda i: (0, 0, i)),
                   pl.BlockSpec((4 * ys * rows, n * cols), lambda i: (i, 0))),
        compiler_params=pltpu.CompilerParams(vmem_limit_bytes=24 * 1024 * 1024),
        name="widen",
    )(own, gathered, gathered)


def shards(tag_ids, tag_amounts, tag_table, position_table, prefix_weight,
           query_own, key_own, value_own, out_grad, seq_lengths):
    tokens = (query_own, key_own, value_own, out_grad)
    prefix, hidden, own_out, own_pg, own_bad, *ahead, me = encode(
        seq_lengths, tag_ids, tag_amounts, tag_table, position_table, prefix_weight, *tokens)
    attn_out, pgrads, *_ = attention(me, seq_lengths, *tokens, prefix, own_out, own_pg, own_bad, ahead)
    prefix_grad, weight_grad = finish(*exchange(hidden, pgrads))
    return attn_out, prefix_grad, weight_grad


def solution(mesh):
    return jax.shard_map(
        shards,
        mesh=mesh,
        in_specs=(
            P(("dp", "tensor"), None),
            P(("dp", "tensor"), None),
            P(),
            P(),
            P(),
            P("dp", None, "tensor"),
            P("dp", None, "tensor"),
            P("dp", None, "tensor"),
            P("dp", None, "tensor"),
            P("dp"),
        ),
        out_specs=(P("dp", None, "tensor"), P(("dp", "tensor"), None, None), P()),
        check_vma=False,
    )
```

```python
import functools
import jax
import jax.numpy as jnp
from jax import lax
from jax.experimental import pallas as pl
from jax.experimental.pallas import tpu as pltpu
from jax.sharding import PartitionSpec as P

HD = 128
SEQS = 128
F32 = jnp.float32
BF16 = jnp.bfloat16
SCALE = 1.0 / HD**0.5
LOG2E = 1.4426950408889634
NT = (((1,), (1,)), ((), ()))
TN = (((0,), (0,)), ((), ()))
MESH = pl.DeviceIdType.MESH


def dot(a, b, dims=(((1,), (0,)), ((), ()))):
    return lax.dot_general(a, b, dims, preferred_element_type=F32)


def in_hbm(*arrays):
    return [pltpu.with_memory_space_constraint(a, pltpu.HBM) for a in arrays]


def hidden_of(mixture, table, pos):
    pooled = jnp.dot(mixture, table.astype(F32), precision=lax.Precision.HIGHEST, preferred_element_type=F32)
    pos = pos.astype(F32)
    return jnp.concatenate([jnp.tanh(pos + pooled[j:j + 1]) for j in range(mixture.shape[0])], 0).astype(BF16)


def attention_scratch(rows, width, plen, sets=()):
    seg_w = width // HD * plen
    return [
        pltpu.VMEM((seg_w + rows, 2 * HD), BF16),
        pltpu.VMEM((seg_w, width), BF16),
        pltpu.VMEM((seg_w, width), BF16),
        pltpu.VMEM((*sets, rows, seg_w), BF16),
        pltpu.VMEM((*sets, rows, seg_w), BF16),
        pltpu.VMEM((rows, seg_w), F32),
    ]


def clear(vx, pkbd, pvbd):
    pkbd[...] = jnp.zeros_like(pkbd)
    pvbd[...] = jnp.zeros_like(pvbd)
    seg_w = pkbd.shape[0]
    vx[0:seg_w, HD:] = jnp.ones((seg_w, HD), BF16)


def place(length, prefix, v, vx, pkbd, pvbd):
    plen, seg_w, rows = prefix.shape[0], pkbd.shape[0], v.shape[0]
    pk, pv = prefix[:, :HD], prefix[:, HD:]
    for h in range(seg_w // plen):
        pkbd[h * plen:(h + 1) * plen, h * HD:(h + 1) * HD] = pk
        pvbd[h * plen:(h + 1) * plen, h * HD:(h + 1) * HD] = pv
        vx[h * plen:(h + 1) * plen, :HD] = pv
    live = lax.broadcasted_iota(jnp.int32, (rows, HD), 0) < length
    vx[seg_w:, :HD] = jnp.where(live, v.astype(F32), 0.0).astype(BF16)
    vx[seg_w:, HD:] = jnp.where(live, 1.0, 0.0).astype(BF16)


def row_delta(g, out, plen):
    heads = g.shape[1] // HD
    seg = lax.broadcasted_iota(jnp.int32, (g.shape[0], heads * plen), 1) // plen
    delta = None
    for h in range(heads):
        lanes = slice(h * HD, (h + 1) * HD)
        total = jnp.sum(g[:, lanes].astype(F32) * out[:, lanes].astype(F32), axis=1, keepdims=True)
        delta = jnp.broadcast_to(total, seg.shape) if h == 0 else jnp.where(seg == h, total, delta)
    return delta


def prefix_gradient(q_ref, g_ref, ds_scr, w_scr, plen):
    heads = q_ref.shape[1] // HD
    for half in range(heads // 2):
        lanes = slice(half * 2 * HD, (half + 1) * 2 * HD)
        dk = dot(ds_scr[...], q_ref[:, lanes], TN)
        dv = dot(w_scr[...], g_ref[:, lanes], TN)
        for i in range(2):
            h = half * 2 + i
            a = dk[h * plen:(h + 1) * plen, i * HD:(i + 1) * HD] * SCALE
            b = dv[h * plen:(h + 1) * plen, i * HD:(i + 1) * HD]
            if h:
                a, b = a + pa, b + pb
            pa, pb = a, b
    return jnp.concatenate([pa, pb], 1)


def attend_fast(length, q_ref, k_ref, g_ref, out_ref, plen, vx, pkbd, pvbd, ds_scr, w_scr, pp_scr,
                beside=None, nr=128, groups=2, late=2):
    rows, width = q_ref.shape
    heads = width // HD
    seg_w = heads * plen
    per = heads // groups
    seg = lax.broadcasted_iota(jnp.int32, (nr, seg_w), 1) // plen
    causal = (lax.broadcasted_iota(jnp.int32, (per * nr, nr), 1)
              <= lax.broadcasted_iota(jnp.int32, (per * nr, nr), 0) % nr)
    c = SCALE * LOG2E

    def score_phase(r0):
        qr = q_ref[r0:r0 + nr]
        pp = jnp.exp2(dot(qr, pkbd[...], NT) * c)
        ppb = pp.astype(BF16)
        zero = jnp.zeros_like(ppb)
        ps = []
        for j in range(groups):
            hs = range(j * per, (j + 1) * per)
            q4 = jnp.concatenate([qr[:, h * HD:(h + 1) * HD] for h in hs], 0)
            parts = [jnp.concatenate([jnp.where(seg == h, ppb, zero) for h in hs], 0)]
            if r0:
                parts.append(jnp.exp2(dot(q4, k_ref[:r0], NT) * c).astype(BF16))
            diag = jnp.exp2(dot(q4, k_ref[r0:r0 + nr], NT) * c)
            parts.append(jnp.where(causal, diag, 0.0).astype(BF16))
            ps.append(jnp.concatenate(parts, 1))
        return pp, ps

    def value_phase(r0, pp, ps, bad):
        invs = []
        os = [dot(p, vx[:seg_w + r0 + nr]) for p in ps]
        for j, o in enumerate(os):
            sums = o[:, HD:]
            ok = (sums > 1e-25) & (sums < 1e25)
            bad = jnp.maximum(bad, jnp.max(jnp.where(ok, 0.0, 1.0).reshape(-1, 8, HD), axis=0))
            inv = 1.0 / sums
            o = (o[:, :HD] * inv).astype(BF16)
            for i in range(per):
                h = j * per + i
                invs.append(inv[i * nr:(i + 1) * nr])
                out_ref[r0:r0 + nr, h * HD:(h + 1) * HD] = o[i * nr:(i + 1) * nr]
        inv_seg = invs[0]
        for h in range(1, heads):
            inv_seg = jnp.where(seg == h, invs[h], inv_seg)
        alive = lax.broadcasted_iota(jnp.int32, (nr, seg_w), 0) + r0 < length
        probs = jnp.where(alive, pp * inv_seg, 0.0)
        w_scr[r0:r0 + nr] = probs.astype(BF16)
        pp_scr[r0:r0 + nr] = probs
        return bad

    bad = jnp.zeros((8, HD), F32)
    starts = list(range(0, rows, nr))
    state = score_phase(starts[0])
    for i, r0 in enumerate(starts):
        now = state
        if i + 1 < len(starts):
            state = score_phase(starts[i + 1])
        if i == 0 and beside is not None:
            beside()
        bad = value_phase(r0, *now, bad)
    step = rows // late
    for r0 in range(0, rows, step):
        g = g_ref[r0:r0 + step]
        delta = row_delta(g, out_ref[r0:r0 + step], plen)
        ds_scr[r0:r0 + step] = (pp_scr[r0:r0 + step] * (dot(g, pvbd[...], NT) - delta)).astype(BF16)
    return bad


def attend_exact(length, q_ref, k_ref, g_ref, out_ref, plen, vx, pkbd, pvbd, ds_scr, w_scr, pp_scr):
    nr = HD
    rows, width = q_ref.shape
    heads = width // HD
    seg_w = heads * plen
    seg = lax.broadcasted_iota(jnp.int32, (nr, seg_w), 1) // plen

    def block(r, carry):
        r0 = pl.multiple_of(r * nr, nr)
        here = pl.ds(r0, nr)
        sp_all = dot(q_ref[here], pkbd[...], NT) * SCALE
        row = lax.broadcasted_iota(jnp.int32, (nr, rows), 0) + r0
        col = lax.broadcasted_iota(jnp.int32, (nr, rows), 1)
        seen = (col <= row) & (col < length)
        pp_scr[here] = jnp.zeros((nr, seg_w), F32)

        def head(h, carry):
            lanes = pl.ds(pl.multiple_of(h * HD, HD), HD)
            s = jnp.where(seen, dot(q_ref[here, lanes], k_ref[...], NT) * SCALE, -1e30)
            sp = jnp.where(seg == h, sp_all, -1e30)
            m = jnp.maximum(jnp.max(s, axis=1, keepdims=True), jnp.max(sp, axis=1, keepdims=True))
            p = jnp.exp(s - m)
            p_pre = jnp.exp(sp - m)
            inv = 1.0 / (jnp.sum(p, axis=1, keepdims=True) + jnp.sum(p_pre, axis=1, keepdims=True))
            p_pre = p_pre * inv
            o = dot((p * inv).astype(BF16), vx[seg_w:, :HD]) + dot(p_pre.astype(BF16), vx[:seg_w, :HD])
            out_ref[here, lanes] = o.astype(BF16)
            pp_scr[here] += p_pre
            return carry

        lax.fori_loop(0, heads, head, 0)
        alive = lax.broadcasted_iota(jnp.int32, (nr, seg_w), 0) + r0 < length
        probs = jnp.where(alive, pp_scr[here], 0.0)
        w_scr[here] = probs.astype(BF16)
        g = g_ref[here]
        ds_scr[here] = (probs * (dot(g, pvbd[...], NT) - row_delta(g, out_ref[here], plen))).astype(BF16)
        return carry

    lax.fori_loop(0, rows // nr, block, 0)


def encode_kernel(n, len_ref, ids_hbm, amt_hbm, table_hbm, pos_hbm, weight_hbm, q_hbm, k_hbm, v_hbm, g_hbm,
                  prefix_ref, hidden_ref, out_ref, pg_ref, bad_ref, nq, nk, nv, ng, me_ref,
                  ids_ref, amt_ref, table_ref, pos_ref, wbuf, q_ref, k_ref, v_ref, g_ref, mine, got,
                  send_sem, recv_sem, load_sem, *scratch):
    d, t = lax.axis_index("dp"), lax.axis_index("tensor")
    me_ref[0] = t
    cols = wbuf.shape[1]
    loads = [pltpu.make_async_copy(src, dst, load_sem.at[i]) for i, (src, dst) in enumerate((
        (ids_hbm, ids_ref), (amt_hbm, amt_ref), (table_hbm, table_ref), (pos_hbm, pos_ref),
        (weight_hbm.at[:, pl.ds(pl.multiple_of(t * cols, cols), cols)], wbuf),
        (q_hbm.at[t], q_ref), (k_hbm.at[t], k_ref), (v_hbm.at[t], v_ref), (g_hbm.at[t], g_ref)))]
    after = lax.rem(t + 1, n)
    ahead = [pltpu.make_async_copy(src.at[after], dst, load_sem.at[9 + i]) for i, (src, dst) in enumerate((
        (q_hbm, nq.at[0]), (k_hbm, nk.at[0]), (v_hbm, nv.at[0]), (g_hbm, ng.at[0])))]
    for load in loads:
        load.start()
    barrier = pltpu.get_barrier_semaphore()
    line = n // 2
    peers = [(d, lax.rem(t // line + a, 2) * line + lax.rem(t + b, line))
             for a, b in ((1, 2), (1, 1), (1, 3), (0, 2), (1, 0), (0, 1), (0, 3))]
    for peer in peers:
        pl.semaphore_signal(barrier, inc=1, device_id=peer, device_id_type=MESH)
    loads[0].wait()
    loads[1].wait()
    tags = table_ref.shape[0]
    lane = lax.broadcasted_iota(jnp.int32, (1, tags), 1)
    ids, amounts = ids_ref[...], amt_ref[...]
    mix = jnp.zeros((1, tags), F32)
    for k in range(ids.shape[1]):
        mix += jnp.where(ids[:, k:k + 1] == lane, amounts[:, k:k + 1], 0.0)
    mix = mix / jnp.sum(amounts, axis=1, keepdims=True)
    mine[...] = jnp.broadcast_to(mix, mine.shape)
    got[t] = jnp.broadcast_to(mix, mine.shape)
    for load in loads[2:5]:
        load.wait()
    plen = pos_ref.shape[0]
    vx, pkbd, pvbd, ds_scr, w_scr, pp_scr = scratch
    length = len_ref[t]
    clear(vx, pkbd, pvbd)
    own = dot(hidden_of(mix, table_ref[...], pos_ref[...]), wbuf[...]).astype(BF16)
    pl.semaphore_wait(barrier, n - 1)
    copies = []
    for i, peer in enumerate(peers):
        copy = pltpu.make_async_remote_copy(
            src_ref=mine, dst_ref=got.at[t], send_sem=send_sem.at[i], recv_sem=recv_sem.at[i],
            device_id=peer, device_id_type=MESH)
        copy.start()
        copies.append(copy)
    for load in loads[5:]:
        load.wait()
    for load in ahead:
        load.start()
    place(length, own, v_ref[...], vx, pkbd, pvbd)
    bad_ref[...] = attend_fast(length, q_ref, k_ref, g_ref, out_ref, plen, *scratch)
    pg_ref[...] = prefix_gradient(q_ref, g_ref, ds_scr, w_scr, plen)
    for copy in copies:
        copy.wait()
    mixture = jnp.concatenate([got[j, 0:1] for j in range(n)], 0)
    hidden = hidden_of(mixture, table_ref[...], pos_ref[...])
    hidden_ref[...] = hidden
    prefix_ref[...] = dot(hidden, wbuf[...]).astype(BF16).reshape(prefix_ref.shape)
    for load in ahead:
        load.wait()


def encode(lengths, tag_ids, tag_amounts, tag_table, position_table, prefix_weight, q, k, v, g):
    n, rows, width = q.shape
    units, total = prefix_weight.shape
    plen = position_table.shape[0]
    cols = total // n
    vmem = pl.BlockSpec(memory_space=pltpu.VMEM)
    smem = pl.BlockSpec(memory_space=pltpu.SMEM)
    return pl.pallas_call(
        functools.partial(encode_kernel, n),
        out_shape=(pltpu.VMEM((n, plen, cols), BF16), pltpu.VMEM((n * plen, units), BF16),
                   pltpu.VMEM((rows, width), BF16), pltpu.VMEM((plen, cols), F32),
                   pltpu.VMEM((8, HD), F32),
                   pltpu.VMEM((3, rows, width), BF16), pltpu.VMEM((3, rows, HD), BF16),
                   pltpu.VMEM((3, rows, HD), BF16), pltpu.VMEM((3, rows, width), BF16),
                   jax.ShapeDtypeStruct((1,), jnp.int32)),
        in_specs=[smem] + [pl.BlockSpec(memory_space=pltpu.HBM)] * 9,
        out_specs=(vmem,) * 9 + (smem,),
        scratch_shapes=[
            pltpu.VMEM(tag_ids.shape, jnp.int32),
            pltpu.VMEM(tag_amounts.shape, F32),
            pltpu.VMEM(tag_table.shape, BF16),
            pltpu.VMEM(position_table.shape, BF16),
            pltpu.VMEM((units, cols), BF16),
            pltpu.VMEM((rows, width), BF16),
            pltpu.VMEM((rows, HD), BF16),
            pltpu.VMEM((rows, HD), BF16),
            pltpu.VMEM((rows, width), BF16),
            pltpu.VMEM((8, tag_table.shape[0]), F32),
            pltpu.VMEM((n, 8, tag_table.shape[0]), F32),
            pltpu.SemaphoreType.DMA((n,)),
            pltpu.SemaphoreType.DMA((n,)),
            pltpu.SemaphoreType.DMA((13,)),
        ] + attention_scratch(rows, width, plen),
        compiler_params=pltpu.CompilerParams(
            collective_id=0, has_side_effects=True, vmem_limit_bytes=24 * 1024 * 1024),
        name="encode",
    )(*in_hbm(lengths, tag_ids, tag_amounts, tag_table, position_table, prefix_weight, q, k, v, g))


def attend_kernel(me_ref, len_ref, prefix_ref, own_out, own_pg, own_bad, _q, _k, _v, _g,
                  q_hbm, k_hbm, v_hbm, g_hbm, out_hbm, pg_ref, qs, ks, vs, gs,
                  outs, bad_scr, rq, rk, rv, rg, out_sem, in_sem, own_sem, redo_sem,
                  vx, pkbd, pvbd, ds_scr, w_scr, pp_scr):
    step, last = pl.program_id(0), pl.num_programs(0) - 1
    me = me_ref[0]
    here = lax.rem(me + 1 + step, last + 2)
    before = lax.rem(me + step, last + 2)
    slot, even = lax.rem(step, 3), lax.rem(step, 2)
    gone = lax.rem(step + 2, 3)
    plen = prefix_ref.shape[1]
    out = outs.at[even]
    own_copy = pltpu.make_async_copy(own_out, out_hbm.at[me], own_sem)

    def loads(example, into):
        return [pltpu.make_async_copy(src.at[example], dst.at[into], in_sem.at[into, i])
                for i, (src, dst) in enumerate(((q_hbm, qs), (k_hbm, ks), (v_hbm, vs), (g_hbm, gs)))]

    def store(into):
        return pltpu.make_async_copy(outs.at[into], out_hbm.at[here], out_sem.at[into])

    @pl.when(step == 0)
    def _():
        own_copy.start()
        clear(vx, pkbd, pvbd)

    @pl.when(step > 0)
    def _():
        for load in loads(here, slot):
            load.wait()

    @pl.when(step < last)
    def _():
        for load in loads(lax.rem(here + 1, last + 2), lax.rem(step + 1, 3)):
            load.start()

    @pl.when(step >= 2)
    def _():
        store(even).wait()

    def previous():
        pg_ref[before] = prefix_gradient(qs.at[gone], gs.at[gone], ds_scr.at[1 - even], w_scr.at[1 - even], plen)

    length = len_ref[here]
    place(length, prefix_ref[here], vs[slot], vx, pkbd, pvbd)
    scratch = (vx, pkbd, pvbd, ds_scr.at[even], w_scr.at[even], pp_scr)
    bad_scr[...] = attend_fast(length, qs.at[slot], ks.at[slot], gs.at[slot], out, plen, *scratch, beside=previous)

    @pl.when(jnp.max(bad_scr[...]) > 0.0)
    def _():
        attend_exact(length, qs.at[slot], ks.at[slot], gs.at[slot], out, plen, *scratch)

    store(even).start()

    @pl.when(step == last)
    def _():
        own_copy.wait()
        pg_ref[here] = prefix_gradient(qs.at[slot], gs.at[slot], ds_scr.at[even], w_scr.at[even], plen)
        pg_ref[me] = own_pg[...]
        store(1 - even).wait()

        @pl.when(jnp.max(own_bad[...]) > 0.0)
        def _():
            copies = [pltpu.make_async_copy(src.at[me], dst, redo_sem.at[i]) for i, (src, dst) in enumerate(
                ((q_hbm, rq), (k_hbm, rk), (v_hbm, rv), (g_hbm, rg)))]
            for copy in copies:
                copy.start()
            for copy in copies:
                copy.wait()
            place(len_ref[me], prefix_ref[me], rv[...], vx, pkbd, pvbd)
            attend_exact(len_ref[me], rq, rk, rg, outs.at[1 - even], plen, *scratch)
            pg_ref[me] = prefix_gradient(rq, rg, ds_scr.at[even], w_scr.at[even], plen)
            again = pltpu.make_async_copy(outs.at[1 - even], out_hbm.at[me], own_sem)
            again.start()
            again.wait()

        store(even).wait()


def attention(me, lengths, q, k, v, g, prefix, own_out, own_pg, own_bad, ahead):
    n, rows, width = q.shape
    plen, cols = prefix.shape[1:]
    smem = pl.BlockSpec(memory_space=pltpu.SMEM)
    vmem = pl.BlockSpec(memory_space=pltpu.VMEM)
    hbm = pl.BlockSpec(memory_space=pltpu.HBM)
    wide, narrow = (rows, width), (rows, HD)
    return pl.pallas_call(
        attend_kernel,
        grid=(n - 1,),
        in_specs=[smem, smem] + [vmem] * 8 + [hbm] * 4,
        out_specs=(hbm,) + (vmem,) * 5,
        scratch_shapes=[
            pltpu.VMEM((2, *wide), BF16),
            pltpu.VMEM((8, HD), F32),
            pltpu.VMEM(wide, BF16),
            pltpu.VMEM(narrow, BF16),
            pltpu.VMEM(narrow, BF16),
            pltpu.VMEM(wide, BF16),
            pltpu.SemaphoreType.DMA((2,)),
            pltpu.SemaphoreType.DMA((3, 4)),
            pltpu.SemaphoreType.DMA,
            pltpu.SemaphoreType.DMA((4,)),
        ] + attention_scratch(rows, width, plen, (2,)),
        out_shape=(pltpu.HBM(q.shape, BF16), pltpu.VMEM((n, plen, cols), F32),
                   *(pltpu.VMEM(buf.shape, BF16) for buf in ahead)),
        input_output_aliases={6 + i: 2 + i for i in range(4)},
        compiler_params=pltpu.CompilerParams(vmem_limit_bytes=40 * 1024 * 1024),
        name="attend",
    )(me, *in_hbm(lengths), prefix, own_out, own_pg, own_bad, *ahead, *in_hbm(q, k, v, g))


def exchange_kernel(hid, pg, own_ref, all_ref, out_buf, part, landed,
                    sems_pg, sems_rs, sems_ag, sems_core):
    d, t = lax.axis_index("dp"), lax.axis_index("tensor")
    y, zh, core = d // 4, lax.rem(d // 2, 2), lax.rem(d, 2)
    zl, x = t // 4, lax.rem(t, 4)
    z = zh * 2 + zl
    me = dict(x=x, y=y, z=z)

    def device(x, y, z, core):
        return ((y * 2 + z // 2) * 2 + core, lax.rem(z, 2) * 4 + x)

    def shifted(offsets, flip=0):
        c = {axis: lax.rem(me[axis] + offsets.get(axis, 0), 4) for axis in me}
        return device(c["x"], c["y"], c["z"], lax.rem(core + flip, 2))

    far = lambda o: -sum((0, 1, 2, 1)[i] for i in o.values())

    def offsets_over(axes):
        out = [{}]
        for axis in axes:
            out = [{**o, axis: i} for o in out for i in range(4)]
        return sorted([o for o in out if any(o.values())], key=far)

    plane, line = offsets_over("xy"), offsets_over("z")
    others = [{"y": i, "z": j} for i in (2, 1, 3, 0) for j in (2, 0) if i or j]
    sums = [(o, flip) for o in others for flip in (0, 1)] + [({}, 1)]
    tensor = [(d, lax.rem(t + i, 8)) for i in range(1, 8)]
    peers = [(far(o), shifted(o)) for o in plane + line]
    peers += [(far(o), shifted(o, flip)) for o, flip in sums if flip or (o["y"] and o["z"])]
    peers += [(-1 - (0, 1, 2, 1)[i], (d, lax.rem(zl + 1, 2) * 4 + lax.rem(x + i, 4))) for i in (1, 2, 3)]
    peers = [peer for _, peer in sorted(peers, key=lambda item: item[0])]
    barrier = pltpu.get_barrier_semaphore()
    for peer in peers:
        pl.semaphore_signal(barrier, inc=1, device_id=peer, device_id_type=MESH)
    grads = pg[...]
    high = grads.astype(BF16)
    out_buf[...] = high
    own_ref[t] = out_buf[t]
    flat_high = high.reshape(-1, high.shape[2])
    low = (grads.reshape(flat_high.shape) - flat_high.astype(F32)).astype(BF16)
    total = dot(hid[...], flat_high, TN) + dot(hid[...], low, TN)
    part[...] = total.astype(BF16).reshape(part.shape)
    pl.semaphore_wait(barrier, len(peers))

    def send(src, dst, sems, i, peer):
        copy = pltpu.make_async_remote_copy(
            src_ref=src, dst_ref=dst, send_sem=sems.at[0, i], recv_sem=sems.at[1, i],
            device_id=peer, device_id_type=MESH)
        copy.start()
        return copy

    scatter = []
    for i, (o, flip) in enumerate(sums):
        to = shifted(o, flip)
        scatter.append(send(part.at[to[0]], landed.at[i], sems_rs, i, to))
    back = [send(out_buf.at[to[1]], own_ref.at[t], sems_pg, i, to) for i, to in enumerate(tensor)]
    chunk = part[d].astype(F32)
    for i, copy in enumerate(scatter):
        copy.wait()
        chunk += landed[i].astype(F32)
    chunk = (chunk * (1.0 / SEQS)).astype(BF16)
    half = chunk.shape[1] // 2
    all_ref[0, core, z, y, x] = chunk[:, :half]
    all_ref[1, core, y, x, z] = chunk[:, half:]
    early = [send(all_ref.at[1, core, y, x, z], all_ref.at[1, core, y, x, z], sems_ag, i, shifted(o))
             for i, o in enumerate(line)]
    first = [send(all_ref.at[0, core, z, y, x], all_ref.at[0, core, z, y, x], sems_ag, 3 + i, shifted(o))
             for i, o in enumerate(plane)]
    for copy in early:
        copy.wait()
    wide = [send(all_ref.at[1, core, y, x], all_ref.at[1, core, y, x], sems_ag, 18 + i, shifted(o))
            for i, o in enumerate(plane)]
    for copy in first:
        copy.wait()
    deep = [send(all_ref.at[0, core, z], all_ref.at[0, core, z], sems_ag, 33 + i, shifted(o))
            for i, o in enumerate(line)]
    sibling = shifted({}, 1)
    passed = [send(all_ref.at[0, core, z], all_ref.at[0, core, z], sems_core, 0, sibling)]
    for o, copy in zip(line, deep):
        copy.wait()
        block = all_ref.at[0, core, lax.rem(z + 4 - o["z"], 4)]
        passed.append(send(block, block, sems_core, o["z"], sibling))
    for i in (2, 1, 3, 0):
        for o, copy in zip(plane, wide):
            if o["y"] == i:
                copy.wait()
        block = all_ref.at[1, core, lax.rem(y + 4 - i, 4)]
        passed.append(send(block, block, sems_core, 4 + i, sibling))
    for copy in passed + back:
        copy.wait()


def exchange(hidden, pgrads):
    n, plen, cols = pgrads.shape
    width = hidden.shape[1]
    rows = width // 16
    vmem = pl.BlockSpec(memory_space=pltpu.VMEM)
    return pl.pallas_call(
        exchange_kernel,
        out_shape=(pltpu.VMEM((n, plen, cols), BF16), pltpu.VMEM((2, 2, 4, 4, 4, rows, cols // 2), BF16)),
        in_specs=[vmem] * 2,
        out_specs=(vmem, vmem),
        scratch_shapes=[
            pltpu.VMEM((n, plen, cols), BF16),
            pltpu.VMEM((16, rows, cols), BF16),
            pltpu.VMEM((16, rows, cols), BF16),
            pltpu.SemaphoreType.DMA((2, 8)),
            pltpu.SemaphoreType.DMA((2, 16)),
            pltpu.SemaphoreType.DMA((2, 36)),
            pltpu.SemaphoreType.DMA((2, 8)),
        ],
        compiler_params=pltpu.CompilerParams(collective_id=1, has_side_effects=True, vmem_limit_bytes=16 * 1024 * 1024),
        name="exchange",
    )(hidden, pgrads)


def finish_kernel(own_ref, first_ref, second_ref, prefix_grad_ref, weight_grad_ref):
    cols = own_ref.shape[2]
    half = cols // 2
    for j in range(own_ref.shape[0]):
        prefix_grad_ref[0, :, j * cols:(j + 1) * cols] = own_ref[j].astype(F32)
    ys, rows = first_ref.shape[3], first_ref.shape[5]
    for y in range(ys):
        for core in range(2):
            for z in range(4):
                r0 = ((y * 2 + z // 2) * 2 + core) * rows
                for x in range(4):
                    c0 = ((z % 2) * 4 + x) * cols
                    weight_grad_ref[r0:r0 + rows, c0:c0 + half] = first_ref[0, core, z, y, x].astype(F32)
                    weight_grad_ref[r0:r0 + rows, c0 + half:c0 + cols] = second_ref[0, core, y, x, z].astype(F32)


def finish(own, gathered, steps=2):
    n, plen, cols = own.shape
    rows = gathered.shape[5]
    ys = 4 // steps
    return pl.pallas_call(
        finish_kernel,
        grid=(steps,),
        out_shape=(pltpu.HBM((1, plen, n * cols), F32), pltpu.HBM((16 * rows, n * cols), F32)),
        in_specs=[pl.BlockSpec((n // steps, plen, cols), lambda i: (i, 0, 0)),
                  pl.BlockSpec((1, 2, 4, ys, 4, rows, cols // 2), lambda i: (0, 0, 0, i, 0, 0, 0)),
                  pl.BlockSpec((1, 2, ys, 4, 4, rows, cols // 2), lambda i: (1, 0, i, 0, 0, 0, 0))],
        out_specs=(pl.BlockSpec((1, plen, n // steps * cols), lambda i: (0, 0, i)),
                   pl.BlockSpec((4 * ys * rows, n * cols), lambda i: (i, 0))),
        compiler_params=pltpu.CompilerParams(vmem_limit_bytes=24 * 1024 * 1024),
        name="widen",
    )(own, gathered, gathered)


def shards(tag_ids, tag_amounts, tag_table, position_table, prefix_weight,
           query_own, key_own, value_own, out_grad, seq_lengths):
    tokens = (query_own, key_own, value_own, out_grad)
    prefix, hidden, own_out, own_pg, own_bad, *ahead, me = encode(
        seq_lengths, tag_ids, tag_amounts, tag_table, position_table, prefix_weight, *tokens)
    attn_out, pgrads, *_ = attention(me, seq_lengths, *tokens, prefix, own_out, own_pg, own_bad, ahead)
    prefix_grad, weight_grad = finish(*exchange(hidden, pgrads))
    return attn_out, prefix_grad, weight_grad


def solution(mesh):
    return jax.shard_map(
        shards,
        mesh=mesh,
        in_specs=(
            P(("dp", "tensor"), None),
            P(("dp", "tensor"), None),
            P(),
            P(),
            P(),
            P("dp", None, "tensor"),
            P("dp", None, "tensor"),
            P("dp", None, "tensor"),
            P("dp", None, "tensor"),
            P("dp"),
        ),
        out_specs=(P("dp", None, "tensor"), P(("dp", "tensor"), None, None), P()),
        check_vma=False,
    )
```
